32 devices in a mesh: scan: 8 (over z, y), lat: 4 (over x, core).
Axes of the slice: x: 2, y: 2, z: 4, core: 2. Of those that a mesh axis runs over, the one named last changes fastest.
Arguments:
- observed: bfloat16 [96, 256, 512], P('scan', 'lat'), may hold values from 0.099609375 to 4
- estimate: float32 [96, 256, 512], P('scan', 'lat'), may hold values from 0.1 to 4
- column_weights: float32 [512, 512], replicated, may hold values from 0 to 0.5, as said below
- plane_taps: float32 [7], replicated, may hold values from 0.1 to 1
- row_taps: float32 [7], replicated, may hold values from 0.1 to 1
- shear_planes: int32 [512], replicated, may hold values from 1 to 95, as said below
Outputs:
- deskewed: float32 [96, 256, 512], P('scan', 'lat')
The draws below stay inside these ranges and needn't reach their ends.
Inputs may be any that keep to these rules, and one draw needn't show every extreme that they name: `shear_planes`: never falls from one column to the next; the first column's offset is 1 and the last column's is 95. `column_weights`: zero more than 8 columns away from the diagonal, positive within.
All inputs are finite; a program needn't handle non-finite values.
Results may differ from the reference program's by a relative error of at most 0.0003.
Values sent between devices are 32-bit elements; how exact they have to be, the bound alone decides.
No kernel may reach another device: no remote copies, remote signals or barrier semaphores. Data moves between devices by JAX's collectives and lax.ppermute only.
A program may use at most 64 MiB of HBM per device.

```python
import math
import jax
import jax.numpy as jnp
from jax import lax

PD = 12
X = 512
PLANE_HALF = 3
ROW_HALF = 3
SKEW = 2
BAND = 8
P_SIZE = 96
Y = 256


def draw_column_weights(key, part):
    values = jnp.exp(jax.random.uniform(key, (X, X), jnp.float32, jnp.log(0.05), jnp.log(0.5)))
    row_ids = jnp.arange(X)[:, None]
    col_ids = jnp.arange(X)[None, :]
    return jnp.where(jnp.abs(row_ids - col_ids) <= BAND, values, 0.0).astype(jnp.float32)


def draw_shear_planes(key, part):
    step_key = jax.random.fold_in(key, 11)
    first_key = jax.random.fold_in(key, 23)
    steps = jax.random.randint(step_key, (X,), 0, 2 * P_SIZE)
    climbed = (jnp.cumsum(steps) - steps[0]) // X
    first = jax.random.randint(first_key, (), 1, PD)
    shaped = jnp.maximum(jnp.minimum(climbed, P_SIZE - 1), first)
    col_ids = jnp.arange(X)
    shaped = jnp.where(col_ids == 0, 1, shaped)
    return jnp.where(col_ids == X - 1, P_SIZE - 1, shaped).astype(jnp.int32)


def level_of(key, dims, pieces, low, top_value):
    loudness = 1.0
    for dim, shards_of in pieces:
        heights = jax.random.uniform(jax.random.fold_in(jax.random.fold_in(key, 6), dim), (shards_of,), jnp.float32, low / len(pieces), top_value / len(pieces))
        loudness = loudness * jnp.repeat(jnp.exp(heights), dims[dim] // shards_of).reshape((-1,) + (1,) * (len(dims) - 1 - dim))
    return loudness


def setup_inputs(seed: int = 0) -> dict:
    key_of = jax.random.split(jax.random.key(seed), 7)
    observed = jnp.clip(jnp.exp(math.log(4.0) - 3.6927934 * jax.random.uniform(key_of[0], (P_SIZE, Y, X), jnp.float32) ** level_of(key_of[0], (P_SIZE, Y, X), ((0, 8), (1, 4)), -0.2, 0.2)), 0.099609375, 4.0).astype(jnp.bfloat16)
    estimate = jnp.clip(jnp.exp(math.log(4.0) - 3.6888794 * jax.random.uniform(key_of[1], (P_SIZE, Y, X), jnp.float32) ** level_of(key_of[1], (P_SIZE, Y, X), ((0, 8), (1, 4)), -0.2, 0.2)), 0.1, 4.0)
    column_weights = draw_column_weights(jax.random.fold_in(key_of[6], 71), 0)
    plane_taps = jnp.clip(jnp.exp(jax.random.uniform(key_of[3], (2 * PLANE_HALF + 1,), jnp.float32, math.log(0.1), math.log(1.0))), 0.1, 1.0)
    row_taps = jnp.clip(jnp.exp(jax.random.uniform(key_of[4], (2 * ROW_HALF + 1,), jnp.float32, math.log(0.1), math.log(1.0))), 0.1, 1.0)
    shear_planes = draw_shear_planes(jax.random.fold_in(key_of[6], 71), 0)
    return {"observed": observed, "estimate": estimate, "column_weights": column_weights, "plane_taps": plane_taps, "row_taps": row_taps, "shear_planes": shear_planes}


def column_mix(field, matrix):
    flat = field.reshape(-1, matrix.shape[0])
    mixed = jnp.dot(flat, matrix, precision=lax.Precision.HIGHEST, preferred_element_type=jnp.float32)
    return mixed.reshape(field.shape)


def row_pass(padded, kernel, direction):
    halfwidth = (kernel.shape[0] - 1) // 2
    row_count = padded.shape[1] - 2 * halfwidth
    summed = jnp.zeros((padded.shape[0], row_count, padded.shape[2]), jnp.float32)
    for offset in range(-halfwidth, halfwidth + 1):
        begin = halfwidth + direction * offset
        summed = summed + kernel[offset + halfwidth] * padded[:, begin:begin + row_count, :]
    return summed


def plane_pass(padded, kernel, direction):
    halfwidth = (kernel.shape[0] - 1) // 2
    plane_count = padded.shape[0] - 2 * halfwidth
    column_count = padded.shape[2]
    widened = jnp.pad(padded, ((0, 0), (0, 0), (halfwidth * SKEW, halfwidth * SKEW)))
    summed = jnp.zeros((plane_count, padded.shape[1], column_count), jnp.float32)
    for offset in range(-halfwidth, halfwidth + 1):
        begin = halfwidth + direction * offset
        column_start = halfwidth * SKEW - direction * offset * SKEW
        summed = summed + kernel[offset + halfwidth] * widened[begin:begin + plane_count, :, column_start:column_start + column_count]
    return summed


def pad_rows(field):
    return jnp.pad(field, ((0, 0), (ROW_HALF, ROW_HALF), (0, 0)))


def pad_planes(field):
    return jnp.pad(field, ((PLANE_HALF, PLANE_HALF), (0, 0), (0, 0)))


def reference(observed, estimate, column_weights, plane_taps, row_taps, shear_planes):
    mixed_cols = column_mix(estimate, column_weights)
    row_blur = row_pass(pad_rows(mixed_cols), row_taps, 1)
    blurred = plane_pass(pad_planes(row_blur), plane_taps, 1)
    quotient = observed.astype(jnp.float32) / blurred
    back_planes = plane_pass(pad_planes(quotient), plane_taps, -1)
    back_rows = row_pass(pad_rows(back_planes), row_taps, -1)
    correction = column_mix(back_rows, column_weights.T)
    updated = estimate * correction
    source_ids = jnp.arange(P_SIZE, dtype=jnp.int32)[:, None] - shear_planes[None, :]
    taken = jnp.take_along_axis(updated, jnp.maximum(source_ids, 0)[:, None, :], axis=0)
    return jnp.where((source_ids >= 0)[:, None, :], taken, 0.0)
```

```python
import functools

import jax
import jax.numpy as jnp
from jax import lax
from jax.experimental import pallas as pl
from jax.experimental.pallas import tpu as pltpu
from jax.sharding import PartitionSpec as P

PLANE_HALF = 3
ROW_HALF = 3
SKEW = 2
LANES = 128
EDGE = 8
F32 = jnp.float32
BF16 = jnp.bfloat16
VMEM = pl.BlockSpec(memory_space=pltpu.VMEM)
SMEM = pl.BlockSpec(memory_space=pltpu.SMEM)
LIMIT = 48 * 1024 * 1024


def run(body, outs, ins, operands, scratch=(), aliases=None, cost=None):
    return pl.pallas_call(
        body,
        out_shape=outs,
        in_specs=ins,
        out_specs=jax.tree.map(lambda _: VMEM, outs),
        scratch_shapes=list(scratch),
        input_output_aliases=aliases or {},
        compiler_params=pltpu.CompilerParams(vmem_limit_bytes=LIMIT),
        cost_estimate=cost,
    )(*operands)


def halves(x):
    high = x.astype(BF16)
    return high, (x - high.astype(F32)).astype(BF16)


def product(x, high_w, low_w, dims):
    high, low = halves(x)
    dot = functools.partial(
        lax.dot_general, dimension_numbers=(dims, ((), ())), preferred_element_type=F32
    )
    return dot(high, high_w) + (dot(high, low_w) + dot(low, high_w))


def fill_rows(pad, top, mid, bottom):
    planes, rows, cols = mid.shape
    pad[:, 0:EDGE, :] = jnp.zeros((planes, EDGE, cols), F32)
    pad[:, EDGE + rows :, :] = jnp.zeros((planes, EDGE, cols), F32)
    pad[:, EDGE - ROW_HALF : EDGE, :] = top[...]
    pad[:, EDGE : EDGE + rows, :] = mid[...]
    pad[:, EDGE + rows : EDGE + rows + ROW_HALF, :] = bottom[...]


def row_sum(pad, plane, rows, taps, direction):
    total = None
    for k in range(2 * ROW_HALF + 1):
        tap = taps[k] if direction > 0 else taps[2 * ROW_HALF - k]
        term = tap * pad[plane, pl.ds(EDGE - ROW_HALF + k, rows), :]
        total = term if total is None else total + term
    return total


def mix_body(est, top, bottom, weights, taps, blur, low3, high3, pad, mixed):
    planes, rows, cols = est.shape
    fill_rows(pad, top, est, bottom)
    high_w, low_w = halves(weights[...])
    group = 4 if planes % 4 == 0 else 1

    def mix(g, _):
        x = pad[pl.ds(g * group, group)].reshape(group * (rows + 2 * EDGE), cols)
        y = product(x, high_w, low_w, ((1,), (0,)))
        mixed[pl.ds(g * group, group)] = y.reshape(group, rows + 2 * EDGE, cols)
        return 0

    lax.fori_loop(0, planes // group, mix, 0)

    def blur_rows(p, _):
        blur[p] = row_sum(mixed, p, rows, taps, 1)
        return 0

    lax.fori_loop(0, planes, blur_rows, 0)
    low3[...] = blur[0:PLANE_HALF]
    high3[...] = blur[planes - PLANE_HALF : planes]


def skewed(x, place):
    rows, cols = x.shape
    wide = jnp.concatenate([x, jnp.zeros((rows, LANES), F32)], axis=1)
    return pltpu.roll(wide, SKEW * place, 1) if place else wide


def unskewed(x, place):
    width = x.shape[1]
    moved = pltpu.roll(x, (width - SKEW * place) % width, 1) if place else x
    return moved[:, : width - LANES]


def plane_sum(field, index, row, taps, direction):
    total = None
    for k in range(2 * PLANE_HALF + 1):
        tap = taps[k] if direction > 0 else taps[2 * PLANE_HALF - k]
        term = tap * field[index + k, pl.ds(row, 8), :]
        total = term if total is None else total + term
    return total


def quotient_body(blur, left, right, observed, taps, ratio, low3, high3, skew, wide):
    planes, rows, cols = blur.shape
    for l in range(PLANE_HALF):
        skew[l] = skewed(left[l], l)
        skew[planes + PLANE_HALF + l] = skewed(right[l], planes + PLANE_HALF + l)
    for l in range(planes):
        skew[PLANE_HALF + l] = skewed(blur[l], PLANE_HALF + l)
        wide[l] = skewed(observed[l].astype(F32), PLANE_HALF + l)

    def plane(l, _):
        place = SKEW * (l + PLANE_HALF)
        lane = lax.broadcasted_iota(jnp.int32, (8, cols + LANES), 1)
        inside = (lane >= place) & (lane < place + cols)

        def tile(t, _):
            row = pl.multiple_of(t * 8, 8)
            blurred = plane_sum(skew, l, row, taps, 1)
            seen = wide[l, pl.ds(row, 8), :]
            ratio[l, pl.ds(row, 8), :] = jnp.where(
                inside, seen / jnp.where(inside, blurred, 1.0), 0.0
            )
            return 0

        return lax.fori_loop(0, rows // 8, tile, 0, unroll=2)

    lax.fori_loop(0, planes, plane, 0)
    for l in range(PLANE_HALF):
        low3[l] = unskewed(ratio[l], PLANE_HALF + l)
        high3[l] = unskewed(ratio[planes - PLANE_HALF + l], planes + l)


def back_body(ratio, left, right, taps, back, top, bottom, skew, wide):
    planes, rows, width = ratio.shape
    for l in range(PLANE_HALF):
        skew[l] = skewed(left[l], l)
        skew[planes + PLANE_HALF + l] = skewed(right[l], planes + PLANE_HALF + l)
    skew[PLANE_HALF : PLANE_HALF + planes] = ratio[...]

    def plane(l, _):
        def tile(t, _):
            row = pl.multiple_of(t * 8, 8)
            wide[l, pl.ds(row, 8), :] = plane_sum(skew, l, row, taps, -1)
            return 0

        return lax.fori_loop(0, rows // 8, tile, 0, unroll=2)

    lax.fori_loop(0, planes, plane, 0)
    for l in range(planes):
        back[l] = unskewed(wide[l], PLANE_HALF + l)
    top[...] = back[:, 0:ROW_HALF, :]
    bottom[...] = back[:, rows - ROW_HALF : rows, :]


def update_body(back, top, bottom, weights, taps, est, turn, out, pad, rows_out):
    planes, rows, cols = est.shape
    fill_rows(pad, top, back, bottom)
    high_w, low_w = halves(weights[...])

    def sum_rows(p, _):
        rows_out[p] = row_sum(pad, p, rows, taps, -1)
        return 0

    lax.fori_loop(0, planes, sum_rows, 0)
    group = 4 if planes % 4 == 0 else 1

    def mix(g, _):
        x = rows_out[pl.ds(g * group, group)].reshape(group * rows, cols)
        y = product(x, high_w, low_w, ((1,), (1,)))
        rows_out[pl.ds(g * group, group)] = y.reshape(group, rows, cols)
        return 0

    lax.fori_loop(0, planes // group, mix, 0)

    def rotate(t, _):
        row = pl.multiple_of(t * 8, 8)
        for c in range(0, cols, 2 * LANES):
            tile = (pl.ds(row, 8), pl.ds(c, 2 * LANES))
            field = [rows_out[(p, *tile)] * est[(p, *tile)] for p in range(planes)]
            bits = jnp.broadcast_to(turn[:, c : c + 2 * LANES], (8, 2 * LANES))
            for bit in range((planes - 1).bit_length()):
                chosen = (bits >> bit & 1) == 1
                field = [
                    jnp.where(chosen, field[(q - (1 << bit)) % planes], field[q])
                    for q in range(planes)
                ]
            for q in range(planes):
                out[(q, *tile)] = field[q]
        return 0

    lax.fori_loop(0, rows // 8, rotate, 0)


class Packing:
    def __init__(self, count, planes, rows, cols):
        self.count, self.planes, self.rows, self.cols = count, planes, rows, cols
        share = max(cols // count, 1)
        self.parts = 2 if rows % 16 == 0 else 1
        self.messages = []
        for d in range(1, count):
            room = share * 5 // 4
            if d == count - 1:
                room = share * 3 // 2
            if d == 1:
                room = share * 9 // 4
            pieces = -(-room // LANES)
            width = min(-(-room // (8 * pieces)) * 8, LANES)
            self.messages.append((d, pieces, width))

    def segments(self, pieces):
        return [
            (m, h, q)
            for m in range(pieces)
            for h in range(self.parts)
            for q in range(self.planes)
        ]

    def shape(self, pieces, width):
        total = pieces * self.parts * self.planes * width
        return (self.rows // self.parts, -(-total // LANES) * LANES)


def lane_of(shape):
    return lax.broadcasted_iota(jnp.int32, shape, 1)


def pack_body(packing, edges, turned, field, *outs):
    plan = packing
    part_rows = plan.rows // plan.parts
    last = plan.cols // LANES - 1
    step = turned[0]

    def tiles(t, _):
        lane = lane_of((8, LANES))
        for (d, pieces, width), out in zip(plan.messages, outs):
            done = {}
            for k, (m, h, q) in enumerate(plan.segments(pieces)):
                low = edges[d * plan.planes + q] + (step * pieces + m) * width
                tile = jnp.minimum(low // LANES, last)
                row = pl.multiple_of(h * part_rows + t * 8, 8)
                first = field[
                    q, pl.ds(row, 8), pl.ds(pl.multiple_of(tile * LANES, LANES), LANES)
                ]
                second = field[
                    q,
                    pl.ds(row, 8),
                    pl.ds(pl.multiple_of(jnp.minimum(tile + 1, last) * LANES, LANES), LANES),
                ]
                begin = k * width
                offset = begin % LANES
                window = jnp.where(lane >= low % LANES, first, second)
                window = pltpu.roll(window, (offset - low) % LANES, 1)
                target = begin // LANES
                done[target] = (
                    window
                    if offset == 0
                    else jnp.where(lane >= offset, window, done[target])
                )
                if offset + width > LANES:
                    done[target + 1] = window
                for full in [x for x in done if (x + 1) * LANES <= begin + width]:
                    out[pl.ds(pl.multiple_of(t * 8, 8), 8), full * LANES : (full + 1) * LANES] = (
                        done.pop(full)
                    )
            for rest in list(done):
                out[pl.ds(pl.multiple_of(t * 8, 8), 8), rest * LANES : (rest + 1) * LANES] = (
                    done.pop(rest)
                )
        return 0

    lax.fori_loop(0, part_rows // 8, tiles, 0)


def unpack_body(packing, first_round, edges, turned, base, *refs):
    plan = packing
    ins, out = refs[:-1], refs[-1]
    part_rows = plan.rows // plan.parts
    count = plan.cols // LANES
    step = turned[0]

    def tiles(t, _):
        lane = lane_of((8, LANES))
        for h in range(plan.parts):
            for q in range(plan.planes):
                rows = pl.ds(pl.multiple_of(h * part_rows + t * 8, 8), 8)
                found = []
                for c in range(count):
                    x = base[q, rows, c * LANES : (c + 1) * LANES]
                    if first_round:
                        x = jnp.where(lane + c * LANES < edges[plan.planes + q], x, 0.0)
                    found.append(x)
                for (d, pieces, width), message in zip(plan.messages, ins):
                    for m in range(pieces):
                        k = plan.segments(pieces).index((m, h, q))
                        low = edges[d * plan.planes + q] + (step * pieces + m) * width
                        high = jnp.minimum(edges[(d + 1) * plan.planes + q], low + width)
                        begin = k * width
                        offset = begin % LANES
                        target = begin // LANES
                        here = pl.ds(pl.multiple_of(t * 8, 8), 8)
                        window = message[here, target * LANES : (target + 1) * LANES]
                        if offset + width > LANES:
                            window = jnp.where(
                                lane >= offset,
                                window,
                                message[here, (target + 1) * LANES : (target + 2) * LANES],
                            )
                        window = pltpu.roll(window, (low - offset) % LANES, 1)
                        for c in range(count):
                            inside = (lane >= low - c * LANES) & (lane < high - c * LANES)
                            found[c] = jnp.where(inside, window, found[c])
                for c in range(count):
                    out[q, rows, c * LANES : (c + 1) * LANES] = found[c]
        return 0

    lax.fori_loop(0, part_rows // 8, tiles, 0)


def to_next(x, axis):
    count = lax.axis_size(axis)
    return lax.ppermute(x, axis, [(i, i + 1) for i in range(count - 1)])


def to_last(x, axis):
    count = lax.axis_size(axis)
    return lax.ppermute(x, axis, [(i + 1, i) for i in range(count - 1)])


def like(*shape):
    return jax.ShapeDtypeStruct(shape, F32)


def on_device(observed, estimate, column_weights, plane_taps, row_taps, shear_planes):
    planes, rows, cols = estimate.shape
    count = lax.axis_size("scan")
    padded = pltpu.VMEM((planes, rows + 2 * EDGE, cols), F32)
    width = cols + LANES
    tall = pltpu.VMEM((planes + 2 * PLANE_HALF, rows, width), F32)
    wide = pltpu.VMEM((planes, rows, width), F32)

    top = to_next(estimate[:, rows - ROW_HALF :, :], "lat")
    bottom = to_last(estimate[:, :ROW_HALF, :], "lat")
    levels = jnp.arange((count + 1) * planes, dtype=jnp.int32) - planes
    edges = jnp.sum(shear_planes[None, :] <= levels[:, None], axis=1, dtype=jnp.int32)
    turn = (shear_planes % planes)[None, :]

    blur, low3, high3 = run(
        mix_body,
        (like(planes, rows, cols), like(PLANE_HALF, rows, cols), like(PLANE_HALF, rows, cols)),
        [VMEM, VMEM, VMEM, VMEM, SMEM],
        (estimate, top, bottom, column_weights, row_taps),
        [padded, padded],
    )
    left, right = to_next(high3, "scan"), to_last(low3, "scan")
    ratio, low3, high3 = run(
        quotient_body,
        (like(planes, rows, width), like(PLANE_HALF, rows, cols), like(PLANE_HALF, rows, cols)),
        [VMEM, VMEM, VMEM, VMEM, SMEM],
        (blur, left, right, observed, plane_taps),
        [tall, wide],
    )
    left, right = to_next(high3, "scan"), to_last(low3, "scan")
    back, top, bottom = run(
        back_body,
        (like(planes, rows, cols), like(planes, ROW_HALF, cols), like(planes, ROW_HALF, cols)),
        [VMEM, VMEM, VMEM, SMEM],
        (ratio, left, right, plane_taps),
        [tall, wide],
    )
    above, below = to_next(bottom, "lat"), to_last(top, "lat")
    turned = run(
        update_body,
        like(planes, rows, cols),
        [VMEM, VMEM, VMEM, VMEM, SMEM, VMEM, VMEM],
        (back, above, below, column_weights, row_taps, estimate, turn),
        [padded, pltpu.VMEM((planes, rows, cols), F32)],
    )

    plan = Packing(count, planes, rows, cols)

    def exchange(step, base, first_round):
        packed = run(
            functools.partial(pack_body, plan),
            tuple(like(*plan.shape(m, w)) for _, m, w in plan.messages),
            [SMEM, SMEM, VMEM],
            (edges, step, turned),
        )
        moved = [
            lax.ppermute(x, "scan", [(i, i + d) for i in range(count - d)])
            for (d, _, _), x in zip(plan.messages, packed)
        ]
        return run(
            functools.partial(unpack_body, plan, first_round),
            like(planes, rows, cols),
            [SMEM, SMEM, VMEM] + [VMEM] * len(moved),
            (edges, step, base, *moved),
        )

    table = edges.reshape(count + 1, planes)
    rooms = jnp.array([m * w for _, m, w in plan.messages], jnp.int32)
    widest = jnp.max(table[2:] - table[1:-1], axis=1)
    rounds = jnp.max((widest + rooms - 1) // rooms)
    first = exchange(jnp.zeros((1,), jnp.int32), turned, True)

    def more(state):
        return state[0] < rounds

    def again(state):
        return state[0] + 1, exchange(state[0][None], state[1], False)

    return lax.while_loop(more, again, (jnp.int32(1), first))[1]


def solution(mesh):
    placed = (P("scan", "lat", None), P("scan", "lat", None), P(), P(), P(), P())
    return jax.shard_map(
        on_device, mesh=mesh, in_specs=placed, out_specs=P("scan", "lat", None), check_vma=False
    )
```

```python
import functools

import jax
import jax.numpy as jnp
from jax import lax
from jax.experimental import pallas as pl
from jax.experimental.pallas import tpu as pltpu
from jax.sharding import PartitionSpec as P

PLANE_HALF = 3
ROW_HALF = 3
SKEW = 2
LANES = 128
LANE_BITS = 7
EDGE = 8
F32 = jnp.float32
BF16 = jnp.bfloat16
VMEM = pl.BlockSpec(memory_space=pltpu.VMEM)
SMEM = pl.BlockSpec(memory_space=pltpu.SMEM)
LIMIT = 20 * 1024 * 1024


def run(body, outs, ins, operands, scratch=(), aliases=None, cost=None):
    return pl.pallas_call(
        body,
        out_shape=outs,
        in_specs=ins,
        out_specs=jax.tree.map(lambda _: VMEM, outs),
        scratch_shapes=list(scratch),
        input_output_aliases=aliases or {},
        compiler_params=pltpu.CompilerParams(vmem_limit_bytes=LIMIT),
        cost_estimate=cost,
    )(*operands)


def halves(x):
    high = x.astype(BF16)
    return high, (x - high.astype(F32)).astype(BF16)


def product(x, high_w, low_w, dims):
    high, low = halves(x)
    dot = functools.partial(
        lax.dot_general, dimension_numbers=(dims, ((), ())), preferred_element_type=F32
    )
    return dot(high, high_w) + (dot(high, low_w) + dot(low, high_w))


def row_sum(field, plane, rows, taps, direction):
    total = None
    for k in range(2 * ROW_HALF + 1):
        tap = taps[k] if direction > 0 else taps[2 * ROW_HALF - k]
        term = tap * field[plane, pl.ds(k, rows), :]
        total = term if total is None else total + term
    return total


def strip_body(est, observed, upper, lower):
    planes, rows, cols = est.shape
    reach = 2 * ROW_HALF
    for l in range(planes):
        seek = (2 * planes + l) * ROW_HALF
        upper[l * reach : (l + 1) * reach, :] = est[l, 0:reach, :]
        lower[l * reach : (l + 1) * reach, :] = est[l, rows - reach : rows, :]
        seen = observed[l].astype(F32)
        upper[seek : seek + ROW_HALF, :] = seen[0:ROW_HALF]
        lower[seek : seek + ROW_HALF, :] = seen[rows - ROW_HALF : rows]


def own_body(est, weights, mixed, high_w, low_w):
    planes, rows, cols = est.shape
    high, low = halves(weights[...])
    high_w[...] = high
    low_w[...] = low
    x = est[...].reshape(planes * rows, cols)
    mixed[...] = product(x, high, low, ((1,), (0,))).reshape(planes, rows, cols)


def rim_body(chunks, place_of, mixed, above, below, high_w, low_w, taps, tall, *refs):
    rims, ends, edge = refs[:-2], refs[-2], refs[-1]
    odd = (place_of[0] & 1) == 1
    planes, rows, cols = mixed.shape
    reach = 2 * ROW_HALF
    ends[...] = jnp.zeros(ends.shape, F32)
    for l in range(planes):
        ends[l, 0:reach, :] = above[l * reach : (l + 1) * reach, :]
        ends[l, EDGE : EDGE + reach, :] = below[l * reach : (l + 1) * reach, :]
    x = ends[...].reshape(planes * 2 * EDGE, cols)
    ends[...] = product(x, high_w[...], low_w[...], ((1,), (0,))).reshape(ends.shape)
    tall[:, 0:reach, :] = ends[:, 0:reach, :]
    tall[:, reach : reach + rows, :] = mixed[...]
    tall[:, reach + rows : reach + rows + EDGE, :] = ends[:, EDGE:, :]
    tall[:, reach + rows + EDGE :, :] = jnp.zeros((planes, EDGE - reach, cols), F32)
    for l in range(PLANE_HALF):
        for side, base in enumerate((0, planes - PLANE_HALF)):
            edge[side] = row_sum(tall, base + l, rows + EDGE, taps, 1)
        for i, (begin, end) in enumerate(chunks):
            low, high = edge[0, begin:end, :], edge[1, begin:end, :]
            rims[2 * i][l] = jnp.where(odd, low, high)
            rims[2 * i + 1][l] = jnp.where(odd, high, low)


def frame_body(tall, observed, above, below, taps, blur, seen, frame):
    planes, rows, cols = observed.shape
    for l in range(planes):
        blur[l] = skewed(row_sum(tall, l, rows + EDGE, taps, 1), PLANE_HALF + l)
    frame[...] = jnp.zeros(frame.shape, F32)
    for l in range(planes):
        seek = (2 * planes + l) * ROW_HALF
        frame[0:ROW_HALF, :] = above[seek : seek + ROW_HALF, :]
        frame[ROW_HALF : ROW_HALF + rows, :] = observed[l].astype(F32)
        frame[ROW_HALF + rows : 2 * ROW_HALF + rows, :] = below[seek : seek + ROW_HALF, :]
        seen[l] = skewed(frame[...], PLANE_HALF + l)


def skewed(x, place):
    rows, cols = x.shape
    wide = jnp.concatenate([x, jnp.zeros((rows, LANES), F32)], axis=1)
    return pltpu.roll(wide, SKEW * place, 1) if place else wide


def unskewed(x, place):
    width = x.shape[1]
    moved = pltpu.roll(x, (width - SKEW * place) % width, 1) if place else x
    return moved[:, : width - LANES]


def set_sides(sides, pair, other, planes, odd):
    for l in range(PLANE_HALF):
        x, y = pair[l], other[l]
        sides[l] = skewed(jnp.where(odd, x, y), l)
        sides[PLANE_HALF + l] = skewed(jnp.where(odd, y, x), planes + PLANE_HALF + l)


def plane_sum(own, own_row, sides, row, plane, planes, taps, direction):
    total = None
    for k in range(2 * PLANE_HALF + 1):
        source = plane + k - PLANE_HALF
        if source < 0:
            x = sides[source + PLANE_HALF, pl.ds(row, 8), :]
        elif source >= planes:
            x = sides[source - planes + PLANE_HALF, pl.ds(row, 8), :]
        else:
            x = own[source, pl.ds(own_row, 8), :]
        term = (taps[k] if direction > 0 else taps[2 * PLANE_HALF - k]) * x
        total = term if total is None else total + term
    return total


def quotient_body(first, begin, size, place_of, blur, seen, left, right, plane_taps, row_taps, *refs):
    odd = (place_of[0] & 1) == 1
    refs = list(refs)
    before = None if first else refs.pop(0)
    spread, pair, other, tail, sides, ratio = refs
    planes = blur.shape[0]
    fresh = 0 if first else EDGE
    if not first:
        ratio[:, 0:EDGE, :] = before[...]
    set_sides(sides, left, right, planes, odd)
    for l in range(planes):

        def tile(t, _, l=l):
            row = pl.multiple_of(t * 8, 8)
            there = pl.multiple_of(row + begin + fresh, 8)
            blurred = plane_sum(blur, there, sides, row, l, planes, plane_taps, 1)
            ratio[l, pl.ds(pl.multiple_of(row + fresh, 8), 8), :] = seen[
                l, pl.ds(there, 8), :
            ] / jnp.where(blurred > 0, blurred, 1.0)
            return 0

        lax.fori_loop(0, (size + EDGE - fresh) // 8, tile, 0)

    def sum_rows(p, _):
        spread[p] = row_sum(ratio, p, size, row_taps, -1)
        return 0

    lax.fori_loop(0, planes, sum_rows, 0)
    tail[...] = ratio[:, size : size + EDGE, :]
    for l in range(PLANE_HALF):
        low = unskewed(spread[l], PLANE_HALF + l)
        high = unskewed(spread[planes - PLANE_HALF + l], planes + l)
        pair[l] = jnp.where(odd, low, high)
        other[l] = jnp.where(odd, high, low)


def update_body(
    sends, begin, edges, place_of, taps, spread, left, right, high_w, low_w, est, turn, *refs
):
    refs = list(refs)
    before = [refs.pop(0) for _ in range(1 if begin else 0)]
    turned, outs = refs[0], refs[1:-3]
    sides, wide, back = refs[-3:]
    planes, rows, cols = turned.shape
    set_sides(sides, left, right, planes, (place_of[0] & 1) == 1)
    for l in range(planes):

        def tile(t, _, l=l):
            row = pl.multiple_of(t * 8, 8)
            wide[pl.ds(row, 8), :] = plane_sum(spread, row, sides, row, l, planes, taps, -1)
            return 0

        lax.fori_loop(0, rows // 8, tile, 0)
        back[l] = unskewed(wide[...], PLANE_HALF + l)
    x = back[...].reshape(planes * rows, cols)
    y = product(x, high_w[...], low_w[...], ((1,), (1,)))
    back[...] = y.reshape(planes, rows, cols)

    def rotate(t, _):
        row = pl.multiple_of(t * 8, 8)
        for c in range(0, cols, 2 * LANES):
            here = (pl.ds(row, 8), pl.ds(c, 2 * LANES))
            there = (pl.ds(begin + row, 8), pl.ds(c, 2 * LANES))
            field = [back[(p, *here)] * est[(p, *there)] for p in range(planes)]
            bits = jnp.broadcast_to(turn[:, c : c + 2 * LANES], (8, 2 * LANES))
            for bit in range((planes - 1).bit_length()):
                chosen = (bits >> bit & 1) == 1
                field = [
                    jnp.where(chosen, field[(q - (1 << bit)) % planes], field[q])
                    for q in range(planes)
                ]
            for q in range(planes):
                turned[(q, *here)] = field[q]
        return 0

    lax.fori_loop(0, rows // 8, rotate, 0)
    for (plan, ds, whole), out in zip(sends, outs):
        fields = fields_of(before + [turned] if whole else [turned], plan.part_rows)
        for i, (d, skip) in enumerate(ds):
            pack(plan, edges, d, skip, fields, out, i)


class Packing:
    def __init__(self, planes, cols, parts, part_rows, width):
        self.planes, self.cols, self.parts, self.width = planes, cols, parts, width
        self.part_rows = part_rows
        tiles = -(-parts * planes * width // LANES)
        self.shape = (tiles * part_rows, LANES)


def lane_of(shape):
    return lax.broadcasted_iota(jnp.int32, shape, 1)


def pack(plan, edges, d, skip, fields, out, slot):
    tall = range(0, plan.part_rows, 8)
    last = plan.cols // LANES - 1
    lane = lane_of((8, LANES))
    done = {}
    for k in range(plan.parts * plan.planes):
        h, q = divmod(k, plan.planes)
        field, base = fields[h]
        low = edges[d * plan.planes + q] + skip
        tile = low >> LANE_BITS
        one = pl.multiple_of(jnp.minimum(tile, last) << LANE_BITS, LANES)
        two = pl.multiple_of(jnp.minimum(tile + 1, last) << LANE_BITS, LANES)
        begin = k * plan.width
        target, offset = divmod(begin, LANES)
        turn = (offset - low) & (LANES - 1)
        split = lane >= (low & (LANES - 1))
        windows = []
        for t in tall:
            rows = pl.ds(base + t, 8)
            first, second = (field[q, rows, pl.ds(c, LANES)] for c in (one, two))
            windows.append(pltpu.roll(jnp.where(split, first, second), turn, 1))
        if offset == 0:
            done[target] = windows
        else:
            done[target] = [
                jnp.where(lane >= offset, x, y) for x, y in zip(windows, done[target])
            ]
        if offset + plan.width > LANES:
            done[target + 1] = windows
        end = k + 1 == plan.parts * plan.planes
        for full in [x for x in done if end or (x + 1) * LANES <= begin + plan.width]:
            for t, x in zip(tall, done.pop(full)):
                out[slot, pl.ds(full * plan.part_rows + t, 8), :] = x


def place(sources, edges, me, bases, out, first_round, begin):
    plan = sources[0][0]
    tall = range(0, plan.part_rows, 8)
    count = plan.cols // LANES
    lane = lane_of((8, LANES))
    spots = [(h, t) for h in range(len(bases)) for t in tall]
    for q in range(plan.planes):
        found = {}
        bound = edges[plan.planes + q]
        for c in range(count):
            keep = lane < bound - c * LANES
            for h, t in spots:
                base, row = bases[h]
                x = base[q, row + t : row + t + 8, c * LANES : (c + 1) * LANES]
                found[h, t, c] = jnp.where(keep, x, 0.0) if first_round else x
        for plan, message, slot, d, skip, first_part in sources:
            low = edges[d * plan.planes + q] + skip
            high = jnp.minimum(edges[(d + 1) * plan.planes + q], low + plan.width)
            high = jnp.where(me >= d, high, 0)
            inside = [(lane >= low - c * LANES) & (lane < high - c * LANES) for c in range(count)]
            for h in range(len(bases)):
                k = (first_part + h) * plan.planes + q
                target, offset = divmod(k * plan.width, LANES)
                turn = (low - offset) & (LANES - 1)
                for t in tall:
                    row = target * plan.part_rows + t
                    window = message[slot, pl.ds(row, 8), :]
                    if offset + plan.width > LANES:
                        after = message[slot, pl.ds(row + plan.part_rows, 8), :]
                        window = jnp.where(lane >= offset, window, after)
                    window = pltpu.roll(window, turn, 1)
                    for c in range(count):
                        found[h, t, c] = jnp.where(inside[c], window, found[h, t, c])
        for (h, t, c), x in found.items():
            row = begin + h * plan.part_rows + t
            out[q, row : row + 8, c * LANES : (c + 1) * LANES] = x


def fields_of(refs, part_rows):
    return [(ref, row) for ref in refs for row in range(0, ref.shape[1], part_rows)]


def settle_first(sends, edges, place_of, base, *refs):
    sources = [
        (plan, ref, i, d, skip, 0)
        for (plan, ds, _), ref in zip(sends, refs)
        for i, (d, skip) in enumerate(ds)
    ]
    fields = fields_of([base], sends[0][0].part_rows)
    place(sources, edges, place_of[0], fields, refs[-1], True, 0)


def settle_last(sends, edges, place_of, settled, base, *refs):
    out, begin = refs[-1], settled.shape[1]
    part_rows = sends[0][0].part_rows
    sources, late = [], []
    for (plan, ds, whole), ref in zip(sends, refs):
        for i, (d, skip) in enumerate(ds):
            if whole:
                late.append((plan, ref, i, d, skip, 0))
            sources.append((plan, ref, i, d, skip, begin // part_rows if whole else 0))
    me = place_of[0]
    place(late, edges, me, fields_of([settled], part_rows), out, False, 0)
    place(sources, edges, me, fields_of([base], part_rows), out, True, begin)


def round_pack_body(count, plan, rooms, edges, place_of, step, *refs):
    out, fields = refs[-1], fields_of(refs[:-1], plan.part_rows)
    for d in range(1, count):
        slot = lax.rem(place_of[0] + d, count)
        pack(plan, edges, d, rooms[d - 1] + step[0] * plan.width, fields, out, slot)


def round_place_body(count, plan, rooms, edges, place_of, step, base, message, out):
    me = place_of[0]
    sources = [
        (plan, message, lax.rem(me + count - d, count), d, rooms[d - 1] + step[0] * plan.width, 0)
        for d in range(1, count)
    ]
    place(sources, edges, me, fields_of([base], plan.part_rows), out, False, 0)


def to_next(x, axis):
    count = lax.axis_size(axis)
    return lax.ppermute(x, axis, [(i, i + 1) for i in range(count - 1)])


def to_last(x, axis):
    count = lax.axis_size(axis)
    return lax.ppermute(x, axis, [(i + 1, i) for i in range(count - 1)])


def swaps(begin, count):
    ends = [(i, i + 1) for i in range(begin, count - 1, 2)]
    return ends + [(j, i) for i, j in ends]


def like(*shape):
    return jax.ShapeDtypeStruct(shape, F32)


def on_device(observed, estimate, column_weights, plane_taps, row_taps, shear_planes):
    planes, rows, cols = estimate.shape
    count = lax.axis_size("scan")
    width = cols + LANES
    half = rows // 2
    chunks = [(0, half), (half, rows)]
    fresh = [(begin + EDGE if begin else 0, end + EDGE) for begin, end in chunks]
    reach = 2 * ROW_HALF

    strip = like(3 * ROW_HALF * planes, cols)
    upper, lower = run(strip_body, (strip, strip), [VMEM, VMEM], (estimate, observed))
    above, below = to_next(lower, "lat"), to_last(upper, "lat")
    me = lax.axis_index("scan").astype(jnp.int32)[None]
    levels = jnp.arange((count + 1) * planes, dtype=jnp.int32) - planes
    edges = jnp.sum(shear_planes[None, :] <= levels[:, None], axis=1, dtype=jnp.int32)
    turn = (shear_planes % planes)[None, :]

    weight = jax.ShapeDtypeStruct(column_weights.shape, BF16)
    mixed, high_w, low_w = run(
        own_body,
        (like(planes, rows, cols), weight, weight),
        [VMEM, VMEM],
        (estimate, column_weights),
    )
    tall, *rims = run(
        functools.partial(rim_body, fresh),
        (
            like(planes, rows + 2 * EDGE, cols),
            *(like(PLANE_HALF, e - b, cols) for b, e in fresh for _ in range(2)),
        ),
        [SMEM, VMEM, VMEM, VMEM, VMEM, VMEM, SMEM],
        (me, mixed, above, below, high_w, low_w, row_taps),
        [
            pltpu.VMEM((planes, 2 * EDGE, cols), F32),
            pltpu.VMEM((2, rows + EDGE, cols), F32),
        ],
    )
    framed = like(planes, rows + EDGE, width)
    blur, seen = run(
        frame_body,
        (framed, framed),
        [VMEM, VMEM, VMEM, VMEM, SMEM],
        (tall, observed, above, below, row_taps),
        [pltpu.VMEM((rows + EDGE, cols), F32)],
    )

    def beside(pair, other):
        last = lax.ppermute(other, "scan", swaps(1, count))
        return lax.ppermute(pair, "scan", swaps(0, count)), last

    def beside(pair, other):
        last = lax.ppermute(other, "scan", swaps(1, count))
        return lax.ppermute(pair, "scan", swaps(0, count)), last

    def exchange(message):
        return lax.all_to_all(message, "scan", split_axis=0, concat_axis=0, tiled=True)

    share = max(cols // count, 8)
    part_rows = 16 if half % 16 == 0 else 8

    def packing(height, columns):
        parts = height // part_rows
        return Packing(planes, cols, parts, part_rows, min(-(-columns // 8) * 8, LANES))

    near, far = packing(rows, share * 9 // 8), packing(rows, share * 3 // 2)
    middle = packing(half, share * 5 // 4)
    later = packing(rows, share // 4)
    mid = [(middle, [(d, 0)], False) for d in range(2, count - 1)]
    wide = [
        (near, [(1, 0), (1, near.width)], True),
        (far, [(count - 1, 0)], True),
    ]
    rooms = [2 * near.width] + [middle.width] * (count - 3) + [far.width]

    tail = settled = None
    pieces = []
    left, right = beside(*rims[0:2])
    for i, (begin, end) in enumerate(chunks):
        size = end - begin
        last = i == len(chunks) - 1
        if pieces:
            left, right, pieces[-1] = lax.optimization_barrier((left, right, pieces[-1]))
        before = (tail,) if pieces else ()
        spread, low, high, tail = run(
            functools.partial(quotient_body, i == 0, begin, size),
            (
                like(planes, size, width),
                like(PLANE_HALF, size, cols),
                like(PLANE_HALF, size, cols),
                like(planes, EDGE, width),
            ),
            [SMEM, VMEM, VMEM, VMEM, VMEM, SMEM, SMEM] + [VMEM] * len(before),
            (me, blur, seen, left, right, plane_taps, row_taps, *before),
            [
                pltpu.VMEM((2 * PLANE_HALF, fresh[i][1] - fresh[i][0], width), F32),
                pltpu.VMEM((planes, size + EDGE, width), F32),
            ],
        )
        if last:
            sides = beside(low, high)
        else:
            ahead = lax.optimization_barrier((low, high, *rims[2 * i + 2 : 2 * i + 4]))
            sides = beside(*ahead[:2])
            left, right = beside(*ahead[2:])
        sends = mid + wide if last else mid
        turned, *packed = run(
            functools.partial(update_body, sends, begin),
            (
                like(planes, size, cols),
                *(like(len(ds), *plan.shape) for plan, ds, _ in sends),
            ),
            [SMEM, SMEM, SMEM] + [VMEM] * (7 + len(pieces)),
            (edges, me, plane_taps, spread, *sides, high_w, low_w, estimate, turn, *pieces),
            [
                pltpu.VMEM((2 * PLANE_HALF, size, width), F32),
                pltpu.VMEM((size, width), F32),
                pltpu.VMEM((planes, size, cols), F32),
            ],
        )
        pieces.append(turned)
        moved = [
            lax.ppermute(x, "scan", [(j, j + ds[0][0]) for j in range(count - ds[0][0])])
            for (_, ds, _), x in zip(sends, packed)
        ]
        ready = (settled,) if last else ()
        settled = run(
            functools.partial(settle_last if last else settle_first, sends),
            like(planes, end, cols),
            [SMEM, SMEM] + [VMEM] * (1 + len(ready) + len(moved)),
            (edges, me, *ready, turned, *moved),
        )

    table = edges.reshape(count + 1, planes)
    row = lax.broadcasted_iota(jnp.int32, (count - 1, planes), 0)
    room = jnp.where(row == 0, rooms[0], jnp.where(row == count - 2, rooms[-1], middle.width))
    rest = table[2:] - table[1:-1] - room
    rounds = jnp.max((rest + later.width - 1) // later.width)

    def again(state):
        step = state[0][None]
        message = run(
            functools.partial(round_pack_body, count, later, rooms),
            like(count, *later.shape),
            [SMEM, SMEM, SMEM] + [VMEM] * len(pieces),
            (edges, me, step, *pieces),
        )
        base = run(
            functools.partial(round_place_body, count, later, rooms),
            like(planes, rows, cols),
            [SMEM, SMEM, SMEM, VMEM, VMEM],
            (edges, me, step, state[1], exchange(message)),
        )
        return state[0] + 1, base

    return lax.while_loop(lambda state: state[0] < rounds, again, (jnp.int32(0), settled))[1]


def solution(mesh):
    placed = (P("scan", "lat", None), P("scan", "lat", None), P(), P(), P(), P())
    return jax.shard_map(
        on_device, mesh=mesh, in_specs=placed, out_specs=P("scan", "lat", None), check_vma=False
    )
```

```python
import functools

import jax
import jax.numpy as jnp
from jax import lax
from jax.experimental import pallas as pl
from jax.experimental.pallas import tpu as pltpu
from jax.sharding import PartitionSpec as P

PLANE_HALF = 3
ROW_HALF = 3
SKEW = 2
LANES = 128
LANE_BITS = 7
EDGE = 8
F32 = jnp.float32
BF16 = jnp.bfloat16
VMEM = pl.BlockSpec(memory_space=pltpu.VMEM)
SMEM = pl.BlockSpec(memory_space=pltpu.SMEM)
LIMIT = 20 * 1024 * 1024


def run(body, outs, ins, operands, scratch=(), aliases=None, cost=None):
    return pl.pallas_call(
        body,
        out_shape=outs,
        in_specs=ins,
        out_specs=jax.tree.map(lambda _: VMEM, outs),
        scratch_shapes=list(scratch),
        input_output_aliases=aliases or {},
        compiler_params=pltpu.CompilerParams(vmem_limit_bytes=LIMIT),
        cost_estimate=cost,
    )(*operands)


def halves(x):
    high = x.astype(BF16)
    return high, (x - high.astype(F32)).astype(BF16)


def product(x, high_w, low_w, dims):
    high, low = halves(x)
    dot = functools.partial(
        lax.dot_general, dimension_numbers=(dims, ((), ())), preferred_element_type=F32
    )
    return dot(high, high_w) + (dot(high, low_w) + dot(low, high_w))


def row_sum(field, plane, rows, taps, direction):
    total = None
    for k in range(2 * ROW_HALF + 1):
        tap = taps[k] if direction > 0 else taps[2 * ROW_HALF - k]
        term = tap * field[plane, pl.ds(k, rows), :]
        total = term if total is None else total + term
    return total


def strip_body(place_of, est, observed, pair, other):
    planes, rows, cols = est.shape
    reach = 2 * ROW_HALF
    odd = (place_of[1] & 1) == 1

    def put(begin, size, upper, lower):
        pair[begin : begin + size, :] = jnp.where(odd, upper, lower)
        other[begin : begin + size, :] = jnp.where(odd, lower, upper)

    for l in range(planes):
        put(l * reach, reach, est[l, 0:reach, :], est[l, rows - reach : rows, :])
        seen = observed[l].astype(F32)
        seek = (2 * planes + l) * ROW_HALF
        put(seek, ROW_HALF, seen[0:ROW_HALF], seen[rows - ROW_HALF : rows])


def own_body(est, weights, mixed, high_w, low_w):
    planes, rows, cols = est.shape
    high, low = halves(weights[...])
    high_w[...] = high
    low_w[...] = low
    x = est[...].reshape(planes * rows, cols)
    mixed[...] = product(x, high, low, ((1,), (0,))).reshape(planes, rows, cols)


def rim_body(chunks, place_of, mixed, pair, other, high_w, low_w, taps, tall, *refs):
    rims, ends, edge = refs[:-2], refs[-2], refs[-1]
    odd = (place_of[0] & 1) == 1
    planes, rows, cols = mixed.shape
    reach = 2 * ROW_HALF
    ends[...] = jnp.zeros(ends.shape, F32)
    odd_row = (place_of[1] & 1) == 1
    for l in range(planes):
        x, y = pair[l * reach : (l + 1) * reach, :], other[l * reach : (l + 1) * reach, :]
        ends[l, 0:reach, :] = jnp.where(odd_row, x, y)
        ends[l, EDGE : EDGE + reach, :] = jnp.where(odd_row, y, x)
    x = ends[...].reshape(planes * 2 * EDGE, cols)
    ends[...] = product(x, high_w[...], low_w[...], ((1,), (0,))).reshape(ends.shape)
    tall[:, 0:reach, :] = ends[:, 0:reach, :]
    tall[:, reach : reach + rows, :] = mixed[...]
    tall[:, reach + rows : reach + rows + EDGE, :] = ends[:, EDGE:, :]
    tall[:, reach + rows + EDGE :, :] = jnp.zeros((planes, EDGE - reach, cols), F32)
    for l in range(PLANE_HALF):
        for side, base in enumerate((0, planes - PLANE_HALF)):
            edge[side] = row_sum(tall, base + l, rows + EDGE, taps, 1)
        for i, (begin, end) in enumerate(chunks):
            low, high = edge[0, begin:end, :], edge[1, begin:end, :]
            rims[2 * i][l] = jnp.where(odd, low, high)
            rims[2 * i + 1][l] = jnp.where(odd, high, low)


def frame_body(place_of, tall, observed, pair, other, taps, blur, seen, frame):
    planes, rows, cols = observed.shape
    for l in range(planes):
        blur[l] = skewed(row_sum(tall, l, rows + EDGE, taps, 1), PLANE_HALF + l)
    frame[...] = jnp.zeros(frame.shape, F32)
    odd = (place_of[1] & 1) == 1
    for l in range(planes):
        seek = (2 * planes + l) * ROW_HALF
        x, y = pair[seek : seek + ROW_HALF, :], other[seek : seek + ROW_HALF, :]
        frame[0:ROW_HALF, :] = jnp.where(odd, x, y)
        frame[ROW_HALF : ROW_HALF + rows, :] = observed[l].astype(F32)
        frame[ROW_HALF + rows : 2 * ROW_HALF + rows, :] = jnp.where(odd, y, x)
        seen[l] = skewed(frame[...], PLANE_HALF + l)


def skewed(x, place):
    rows, cols = x.shape
    wide = jnp.concatenate([x, jnp.zeros((rows, LANES), F32)], axis=1)
    return pltpu.roll(wide, SKEW * place, 1) if place else wide


def unskewed(x, place):
    width = x.shape[1]
    moved = pltpu.roll(x, (width - SKEW * place) % width, 1) if place else x
    return moved[:, : width - LANES]


def set_sides(sides, pair, other, planes, odd):
    for l in range(PLANE_HALF):
        x, y = pair[l], other[l]
        sides[l] = skewed(jnp.where(odd, x, y), l)
        sides[PLANE_HALF + l] = skewed(jnp.where(odd, y, x), planes + PLANE_HALF + l)


def plane_sum(own, own_row, sides, row, plane, planes, taps, direction):
    total = None
    for k in range(2 * PLANE_HALF + 1):
        source = plane + k - PLANE_HALF
        if source < 0:
            x = sides[source + PLANE_HALF, pl.ds(row, 8), :]
        elif source >= planes:
            x = sides[source - planes + PLANE_HALF, pl.ds(row, 8), :]
        else:
            x = own[source, pl.ds(own_row, 8), :]
        term = (taps[k] if direction > 0 else taps[2 * PLANE_HALF - k]) * x
        total = term if total is None else total + term
    return total


def quotient_body(first, begin, size, place_of, blur, seen, left, right, plane_taps, row_taps, *refs):
    odd = (place_of[0] & 1) == 1
    refs = list(refs)
    before = None if first else refs.pop(0)
    spread, pair, other, tail, sides, ratio = refs
    planes = blur.shape[0]
    fresh = 0 if first else EDGE
    if not first:
        ratio[:, 0:EDGE, :] = before[...]
    set_sides(sides, left, right, planes, odd)
    for l in range(planes):

        def tile(t, _, l=l):
            row = pl.multiple_of(t * 8, 8)
            there = pl.multiple_of(row + begin + fresh, 8)
            blurred = plane_sum(blur, there, sides, row, l, planes, plane_taps, 1)
            ratio[l, pl.ds(pl.multiple_of(row + fresh, 8), 8), :] = seen[
                l, pl.ds(there, 8), :
            ] / jnp.where(blurred > 0, blurred, 1.0)
            return 0

        lax.fori_loop(0, (size + EDGE - fresh) // 8, tile, 0)

    def sum_rows(p, _):
        spread[p] = row_sum(ratio, p, size, row_taps, -1)
        return 0

    lax.fori_loop(0, planes, sum_rows, 0)
    tail[...] = ratio[:, size : size + EDGE, :]
    for l in range(PLANE_HALF):
        low = unskewed(spread[l], PLANE_HALF + l)
        high = unskewed(spread[planes - PLANE_HALF + l], planes + l)
        pair[l] = jnp.where(odd, low, high)
        other[l] = jnp.where(odd, high, low)


def update_body(
    sends, begin, edges, place_of, taps, spread, left, right, high_w, low_w, est, turn, *refs
):
    refs = list(refs)
    before = [refs.pop(0) for _ in range(1 if begin else 0)]
    turned, outs = refs[0], refs[1:-3]
    sides, wide, back = refs[-3:]
    planes, rows, cols = turned.shape
    set_sides(sides, left, right, planes, (place_of[0] & 1) == 1)
    for l in range(planes):

        def tile(t, _, l=l):
            row = pl.multiple_of(t * 8, 8)
            wide[pl.ds(row, 8), :] = plane_sum(spread, row, sides, row, l, planes, taps, -1)
            return 0

        lax.fori_loop(0, rows // 8, tile, 0)
        back[l] = unskewed(wide[...], PLANE_HALF + l)
    x = back[...].reshape(planes * rows, cols)
    y = product(x, high_w[...], low_w[...], ((1,), (1,)))
    back[...] = y.reshape(planes, rows, cols)

    def rotate(t, _):
        row = pl.multiple_of(t * 8, 8)
        for c in range(0, cols, 2 * LANES):
            here = (pl.ds(row, 8), pl.ds(c, 2 * LANES))
            there = (pl.ds(begin + row, 8), pl.ds(c, 2 * LANES))
            field = [back[(p, *here)] * est[(p, *there)] for p in range(planes)]
            bits = jnp.broadcast_to(turn[:, c : c + 2 * LANES], (8, 2 * LANES))
            for bit in range((planes - 1).bit_length()):
                chosen = (bits >> bit & 1) == 1
                field = [
                    jnp.where(chosen, field[(q - (1 << bit)) % planes], field[q])
                    for q in range(planes)
                ]
            for q in range(planes):
                turned[(q, *here)] = field[q]
        return 0

    lax.fori_loop(0, rows // 8, rotate, 0)
    for (plan, ds, whole), out in zip(sends, outs):
        fields = fields_of(before + [turned] if whole else [turned], plan.part_rows)
        for i, (d, skip) in enumerate(ds):
            pack(plan, edges, d, skip, fields, out, i)


class Packing:
    def __init__(self, planes, cols, parts, part_rows, width):
        self.planes, self.cols, self.parts, self.width = planes, cols, parts, width
        self.part_rows = part_rows
        tiles = -(-parts * planes * width // LANES)
        self.shape = (tiles * part_rows, LANES)


def lane_of(shape):
    return lax.broadcasted_iota(jnp.int32, shape, 1)


def pack(plan, edges, d, skip, fields, out, slot):
    tall = range(0, plan.part_rows, 8)
    last = plan.cols // LANES - 1
    lane = lane_of((8, LANES))
    done = {}
    for k in range(plan.parts * plan.planes):
        h, q = divmod(k, plan.planes)
        field, base = fields[h]
        low = edges[d * plan.planes + q] + skip
        tile = low >> LANE_BITS
        one = pl.multiple_of(jnp.minimum(tile, last) << LANE_BITS, LANES)
        two = pl.multiple_of(jnp.minimum(tile + 1, last) << LANE_BITS, LANES)
        begin = k * plan.width
        target, offset = divmod(begin, LANES)
        turn = (offset - low) & (LANES - 1)
        split = lane >= (low & (LANES - 1))
        windows = []
        for t in tall:
            rows = pl.ds(base + t, 8)
            first, second = (field[q, rows, pl.ds(c, LANES)] for c in (one, two))
            windows.append(pltpu.roll(jnp.where(split, first, second), turn, 1))
        if offset == 0:
            done[target] = windows
        else:
            done[target] = [
                jnp.where(lane >= offset, x, y) for x, y in zip(windows, done[target])
            ]
        if offset + plan.width > LANES:
            done[target + 1] = windows
        end = k + 1 == plan.parts * plan.planes
        for full in [x for x in done if end or (x + 1) * LANES <= begin + plan.width]:
            for t, x in zip(tall, done.pop(full)):
                out[slot, pl.ds(full * plan.part_rows + t, 8), :] = x


def place(sources, edges, me, bases, out, first_round, begin):
    plan = sources[0][0]
    tall = range(0, plan.part_rows, 8)
    count = plan.cols // LANES
    lane = lane_of((8, LANES))
    spots = [(h, t) for h in range(len(bases)) for t in tall]
    for q in range(plan.planes):
        found = {}
        bound = edges[plan.planes + q]
        for c in range(count):
            keep = lane < bound - c * LANES
            for h, t in spots:
                base, row = bases[h]
                x = base[q, row + t : row + t + 8, c * LANES : (c + 1) * LANES]
                found[h, t, c] = jnp.where(keep, x, 0.0) if first_round else x
        for plan, message, slot, d, skip, first_part in sources:
            low = edges[d * plan.planes + q] + skip
            high = jnp.minimum(edges[(d + 1) * plan.planes + q], low + plan.width)
            high = jnp.where(me >= d, high, 0)
            inside = [(lane >= low - c * LANES) & (lane < high - c * LANES) for c in range(count)]
            for h in range(len(bases)):
                k = (first_part + h) * plan.planes + q
                target, offset = divmod(k * plan.width, LANES)
                turn = (low - offset) & (LANES - 1)
                for t in tall:
                    row = target * plan.part_rows + t
                    window = message[slot, pl.ds(row, 8), :]
                    if offset + plan.width > LANES:
                        after = message[slot, pl.ds(row + plan.part_rows, 8), :]
                        window = jnp.where(lane >= offset, window, after)
                    window = pltpu.roll(window, turn, 1)
                    for c in range(count):
                        found[h, t, c] = jnp.where(inside[c], window, found[h, t, c])
        for (h, t, c), x in found.items():
            row = begin + h * plan.part_rows + t
            out[q, row : row + 8, c * LANES : (c + 1) * LANES] = x


def fields_of(refs, part_rows):
    return [(ref, row) for ref in refs for row in range(0, ref.shape[1], part_rows)]


def settle_first(sends, edges, place_of, base, *refs):
    sources = [
        (plan, ref, i, d, skip, 0)
        for (plan, ds, _), ref in zip(sends, refs)
        for i, (d, skip) in enumerate(ds)
    ]
    fields = fields_of([base], sends[0][0].part_rows)
    place(sources, edges, place_of[0], fields, refs[-1], True, 0)


def settle_last(sends, edges, place_of, settled, base, *refs):
    out, begin = refs[-1], settled.shape[1]
    part_rows = sends[0][0].part_rows
    sources, late = [], []
    for (plan, ds, whole), ref in zip(sends, refs):
        for i, (d, skip) in enumerate(ds):
            if whole:
                late.append((plan, ref, i, d, skip, 0))
            sources.append((plan, ref, i, d, skip, begin // part_rows if whole else 0))
    me = place_of[0]
    place(late, edges, me, fields_of([settled], part_rows), out, False, 0)
    place(sources, edges, me, fields_of([base], part_rows), out, True, begin)


def round_pack_body(count, plan, rooms, edges, place_of, step, *refs):
    out, fields = refs[-1], fields_of(refs[:-1], plan.part_rows)
    for d in range(1, count):
        slot = lax.rem(place_of[0] + d, count)
        pack(plan, edges, d, rooms[d - 1] + step[0] * plan.width, fields, out, slot)


def round_place_body(count, plan, rooms, edges, place_of, step, base, message, out):
    me = place_of[0]
    sources = [
        (plan, message, lax.rem(me + count - d, count), d, rooms[d - 1] + step[0] * plan.width, 0)
        for d in range(1, count)
    ]
    place(sources, edges, me, fields_of([base], plan.part_rows), out, False, 0)


def swapped(x, axis, begin):
    ends = [(i, i + 1) for i in range(begin, lax.axis_size(axis) - 1, 2)]
    return lax.ppermute(x, axis, ends + [(j, i) for i, j in ends])


def like(*shape):
    return jax.ShapeDtypeStruct(shape, F32)


def on_device(observed, estimate, column_weights, plane_taps, row_taps, shear_planes):
    planes, rows, cols = estimate.shape
    count = lax.axis_size("scan")
    width = cols + LANES
    half = rows * 4 // 64 * 8
    chunks = [(0, half), (half, rows)]
    fresh = [(begin + EDGE if begin else 0, end + EDGE) for begin, end in chunks]
    reach = 2 * ROW_HALF

    strip = like(3 * ROW_HALF * planes, cols)
    me = jnp.stack([lax.axis_index("scan"), lax.axis_index("lat")]).astype(jnp.int32)
    pair, other = run(strip_body, (strip, strip), [SMEM, VMEM, VMEM], (me, estimate, observed))
    below = swapped(other, "lat", 1)
    above = swapped(pair, "lat", 0)
    levels = jnp.arange((count + 1) * planes, dtype=jnp.int32) - planes
    edges = jnp.sum(shear_planes[None, :] <= levels[:, None], axis=1, dtype=jnp.int32)
    turn = (shear_planes % planes)[None, :]

    weight = jax.ShapeDtypeStruct(column_weights.shape, BF16)
    mixed, high_w, low_w = run(
        own_body,
        (like(planes, rows, cols), weight, weight),
        [VMEM, VMEM],
        (estimate, column_weights),
    )
    tall, *rims = run(
        functools.partial(rim_body, fresh),
        (
            like(planes, rows + 2 * EDGE, cols),
            *(like(PLANE_HALF, e - b, cols) for b, e in fresh for _ in range(2)),
        ),
        [SMEM, VMEM, VMEM, VMEM, VMEM, VMEM, SMEM],
        (me, mixed, above, below, high_w, low_w, row_taps),
        [
            pltpu.VMEM((planes, 2 * EDGE, cols), F32),
            pltpu.VMEM((2, rows + EDGE, cols), F32),
        ],
    )
    framed = like(planes, rows + EDGE, width)
    blur, seen = run(
        frame_body,
        (framed, framed),
        [SMEM, VMEM, VMEM, VMEM, VMEM, SMEM],
        (me, tall, observed, above, below, row_taps),
        [pltpu.VMEM((rows + EDGE, cols), F32)],
    )

    def beside(pair, other):
        last = swapped(other, "scan", 1)
        return swapped(pair, "scan", 0), last

    def beside(pair, other):
        last = swapped(other, "scan", 1)
        return swapped(pair, "scan", 0), last

    def exchange(message):
        return lax.all_to_all(message, "scan", split_axis=0, concat_axis=0, tiled=True)

    share = max(cols // count, 8)
    part_rows = 16 if half % 16 == 0 and rows % 16 == 0 else 8

    def packing(height, columns):
        parts = height // part_rows
        return Packing(planes, cols, parts, part_rows, min(-(-columns // 8) * 8, LANES))

    near, far = packing(rows, share * 9 // 8), packing(rows, share * 3 // 2)
    later = packing(rows, share // 4)
    mids = []
    for begin, end in chunks:
        middle = packing(end - begin, share * 5 // 4)
        middle_first = sorted(range(2, count - 1), key=lambda d: abs(2 * d - count - 1))
        distances = middle_first if begin else range(2, count - 1)
        mids.append([(middle, [(d, 0)], False) for d in distances])
    wide = [
        (near, [(1, 0), (1, near.width)], True),
        (far, [(count - 1, 0)], True),
    ]
    rooms = [2 * near.width] + [middle.width] * (count - 3) + [far.width]

    tail = settled = None
    pieces = []
    left, right = beside(*rims[0:2])
    for i, (begin, end) in enumerate(chunks):
        size = end - begin
        last = i == len(chunks) - 1
        if pieces:
            left, right, pieces[-1] = lax.optimization_barrier((left, right, pieces[-1]))
        before = (tail,) if pieces else ()
        spread, low, high, tail = run(
            functools.partial(quotient_body, i == 0, begin, size),
            (
                like(planes, size, width),
                like(PLANE_HALF, size, cols),
                like(PLANE_HALF, size, cols),
                like(planes, EDGE, width),
            ),
            [SMEM, VMEM, VMEM, VMEM, VMEM, SMEM, SMEM] + [VMEM] * len(before),
            (me, blur, seen, left, right, plane_taps, row_taps, *before),
            [
                pltpu.VMEM((2 * PLANE_HALF, fresh[i][1] - fresh[i][0], width), F32),
                pltpu.VMEM((planes, size + EDGE, width), F32),
            ],
        )
        if last:
            heavy = [j for j, (_, ds, _) in enumerate(mids[0]) if abs(2 * ds[0][0] - count) == 2]
            rest = [j for j in range(len(mids[0])) if j not in heavy]
            low, high, early = lax.optimization_barrier((low, high, [moved[j] for j in heavy]))
            sides = beside(low, high)
            sides, late = lax.optimization_barrier((sides, [moved[j] for j in rest]))
            moved = [None] * len(mids[0])
            for j, x in zip(heavy + rest, early + late):
                moved[j] = x
            settled = run(
                functools.partial(settle_first, mids[0]),
                like(planes, begin, cols),
                [SMEM, SMEM] + [VMEM] * (1 + len(moved)),
                (edges, me, pieces[0], *moved),
            )
        else:
            ahead = lax.optimization_barrier((low, high, *rims[2 * i + 2 : 2 * i + 4]))
            sides = beside(*ahead[:2])
            left, right = beside(*ahead[2:])
        sends = mids[i] + wide if last else mids[i]
        turned, *packed = run(
            functools.partial(update_body, sends, begin),
            (
                like(planes, size, cols),
                *(like(len(ds), *plan.shape) for plan, ds, _ in sends),
            ),
            [SMEM, SMEM, SMEM] + [VMEM] * (7 + len(pieces)),
            (edges, me, plane_taps, spread, *sides, high_w, low_w, estimate, turn, *pieces),
            [
                pltpu.VMEM((2 * PLANE_HALF, size, width), F32),
                pltpu.VMEM((size, width), F32),
                pltpu.VMEM((planes, size, cols), F32),
            ],
        )
        pieces.append(turned)
        moved = [
            lax.ppermute(x, "scan", [(j, j + ds[0][0]) for j in range(count - ds[0][0])])
            for (_, ds, _), x in zip(sends, packed)
        ]
    settled = run(
        functools.partial(settle_last, sends),
        like(planes, rows, cols),
        [SMEM, SMEM] + [VMEM] * (2 + len(moved)),
        (edges, me, settled, turned, *moved),
    )

    table = edges.reshape(count + 1, planes)
    row = lax.broadcasted_iota(jnp.int32, (count - 1, planes), 0)
    room = jnp.where(row == 0, rooms[0], jnp.where(row == count - 2, rooms[-1], middle.width))
    rest = table[2:] - table[1:-1] - room
    rounds = jnp.max((rest + later.width - 1) // later.width)

    def again(state):
        step = state[0][None]
        message = run(
            functools.partial(round_pack_body, count, later, rooms),
            like(count, *later.shape),
            [SMEM, SMEM, SMEM] + [VMEM] * len(pieces),
            (edges, me, step, *pieces),
        )
        base = run(
            functools.partial(round_place_body, count, later, rooms),
            like(planes, rows, cols),
            [SMEM, SMEM, SMEM, VMEM, VMEM],
            (edges, me, step, state[1], exchange(message)),
        )
        return state[0] + 1, base

    return lax.while_loop(lambda state: state[0] < rounds, again, (jnp.int32(0), settled))[1]


def solution(mesh):
    placed = (P("scan", "lat", None), P("scan", "lat", None), P(), P(), P(), P())
    return jax.shard_map(
        on_device, mesh=mesh, in_specs=placed, out_specs=P("scan", "lat", None), check_vma=False
    )
```

```python
import functools

import jax
import jax.numpy as jnp
from jax import lax
from jax.experimental import pallas as pl
from jax.experimental.pallas import tpu as pltpu
from jax.sharding import PartitionSpec as P

PLANE_HALF = 3
ROW_HALF = 3
SKEW = 2
LANES = 128
LANE_BITS = 7
EDGE = 8
F32 = jnp.float32
BF16 = jnp.bfloat16
VMEM = pl.BlockSpec(memory_space=pltpu.VMEM)
SMEM = pl.BlockSpec(memory_space=pltpu.SMEM)
LIMIT = 20 * 1024 * 1024


def run(body, outs, ins, operands, scratch=(), aliases=None, cost=None):
    return pl.pallas_call(
        body,
        out_shape=outs,
        in_specs=ins,
        out_specs=jax.tree.map(lambda _: VMEM, outs),
        scratch_shapes=list(scratch),
        input_output_aliases=aliases or {},
        compiler_params=pltpu.CompilerParams(vmem_limit_bytes=LIMIT),
        cost_estimate=cost,
    )(*operands)


def halves(x):
    high = x.astype(BF16)
    return high, (x - high.astype(F32)).astype(BF16)


def product(x, high_w, low_w, dims):
    high, low = halves(x)
    dot = functools.partial(
        lax.dot_general, dimension_numbers=(dims, ((), ())), preferred_element_type=F32
    )
    return dot(high, high_w) + (dot(high, low_w) + dot(low, high_w))


def row_sum(field, plane, rows, taps, direction):
    total = None
    for k in range(2 * ROW_HALF + 1):
        tap = taps[k] if direction > 0 else taps[2 * ROW_HALF - k]
        term = tap * field[plane, pl.ds(k, rows), :]
        total = term if total is None else total + term
    return total


def strip_body(place_of, est, observed, pair, other):
    planes, rows, cols = est.shape
    reach = 2 * ROW_HALF
    odd = (place_of[1] & 1) == 1

    def put(begin, size, upper, lower):
        pair[begin : begin + size, :] = jnp.where(odd, upper, lower)
        other[begin : begin + size, :] = jnp.where(odd, lower, upper)

    for l in range(planes):
        put(l * reach, reach, est[l, 0:reach, :], est[l, rows - reach : rows, :])
        seen = observed[l].astype(F32)
        seek = (2 * planes + l) * ROW_HALF
        put(seek, ROW_HALF, seen[0:ROW_HALF], seen[rows - ROW_HALF : rows])


def own_body(est, weights, mixed, high_w, low_w):
    planes, rows, cols = est.shape
    high, low = halves(weights[...])
    high_w[...] = high
    low_w[...] = low
    x = est[...].reshape(planes * rows, cols)
    mixed[...] = product(x, high, low, ((1,), (0,))).reshape(planes, rows, cols)


def rim_body(chunks, place_of, mixed, pair, other, high_w, low_w, taps, tall, *refs):
    rims, ends, edge = refs[:-2], refs[-2], refs[-1]
    odd = (place_of[0] & 1) == 1
    planes, rows, cols = mixed.shape
    reach = 2 * ROW_HALF
    ends[...] = jnp.zeros(ends.shape, F32)
    odd_row = (place_of[1] & 1) == 1
    for l in range(planes):
        x, y = pair[l * reach : (l + 1) * reach, :], other[l * reach : (l + 1) * reach, :]
        ends[l, 0:reach, :] = jnp.where(odd_row, x, y)
        ends[l, EDGE : EDGE + reach, :] = jnp.where(odd_row, y, x)
    x = ends[...].reshape(planes * 2 * EDGE, cols)
    ends[...] = product(x, high_w[...], low_w[...], ((1,), (0,))).reshape(ends.shape)
    tall[:, 0:reach, :] = ends[:, 0:reach, :]
    tall[:, reach : reach + rows, :] = mixed[...]
    tall[:, reach + rows : reach + rows + EDGE, :] = ends[:, EDGE:, :]
    tall[:, reach + rows + EDGE :, :] = jnp.zeros((planes, EDGE - reach, cols), F32)
    for l in range(PLANE_HALF):
        for side, base in enumerate((0, planes - PLANE_HALF)):
            edge[side] = row_sum(tall, base + l, rows + EDGE, taps, 1)
        for i, (begin, end) in enumerate(chunks):
            low, high = edge[0, begin:end, :], edge[1, begin:end, :]
            rims[2 * i][l] = jnp.where(odd, low, high)
            rims[2 * i + 1][l] = jnp.where(odd, high, low)


def frame_body(place_of, tall, observed, pair, other, taps, blur, seen, frame):
    planes, rows, cols = observed.shape
    for l in range(planes):
        blur[l] = skewed(row_sum(tall, l, rows + EDGE, taps, 1), PLANE_HALF + l)
    frame[...] = jnp.zeros(frame.shape, F32)
    odd = (place_of[1] & 1) == 1
    for l in range(planes):
        seek = (2 * planes + l) * ROW_HALF
        x, y = pair[seek : seek + ROW_HALF, :], other[seek : seek + ROW_HALF, :]
        frame[0:ROW_HALF, :] = jnp.where(odd, x, y)
        frame[ROW_HALF : ROW_HALF + rows, :] = observed[l].astype(F32)
        frame[ROW_HALF + rows : 2 * ROW_HALF + rows, :] = jnp.where(odd, y, x)
        seen[l] = skewed(frame[...], PLANE_HALF + l)


def skewed(x, place):
    rows, cols = x.shape
    wide = jnp.concatenate([x, jnp.zeros((rows, LANES), F32)], axis=1)
    return pltpu.roll(wide, SKEW * place, 1) if place else wide


def unskewed(x, place):
    width = x.shape[1]
    moved = pltpu.roll(x, (width - SKEW * place) % width, 1) if place else x
    return moved[:, : width - LANES]


def set_sides(sides, pair, other, planes, odd):
    for l in range(PLANE_HALF):
        x, y = pair[l], other[l]
        sides[l] = skewed(jnp.where(odd, x, y), l)
        sides[PLANE_HALF + l] = skewed(jnp.where(odd, y, x), planes + PLANE_HALF + l)


def plane_sum(own, own_row, sides, row, plane, planes, taps, direction):
    total = None
    for k in range(2 * PLANE_HALF + 1):
        source = plane + k - PLANE_HALF
        if source < 0:
            x = sides[source + PLANE_HALF, pl.ds(row, 8), :]
        elif source >= planes:
            x = sides[source - planes + PLANE_HALF, pl.ds(row, 8), :]
        else:
            x = own[source, pl.ds(own_row, 8), :]
        term = (taps[k] if direction > 0 else taps[2 * PLANE_HALF - k]) * x
        total = term if total is None else total + term
    return total


def quotient_body(first, begin, size, place_of, blur, seen, left, right, plane_taps, row_taps, *refs):
    odd = (place_of[0] & 1) == 1
    refs = list(refs)
    before = None if first else refs.pop(0)
    spread, pair, other, tail, sides, ratio = refs
    planes = blur.shape[0]
    fresh = 0 if first else EDGE
    if not first:
        ratio[:, 0:EDGE, :] = before[...]
    set_sides(sides, left, right, planes, odd)
    for l in range(planes):

        def tile(t, _, l=l):
            row = pl.multiple_of(t * 8, 8)
            there = pl.multiple_of(row + begin + fresh, 8)
            blurred = plane_sum(blur, there, sides, row, l, planes, plane_taps, 1)
            ratio[l, pl.ds(pl.multiple_of(row + fresh, 8), 8), :] = seen[
                l, pl.ds(there, 8), :
            ] / jnp.where(blurred > 0, blurred, 1.0)
            return 0

        lax.fori_loop(0, (size + EDGE - fresh) // 8, tile, 0, unroll=True)

    def sum_rows(p, _):
        spread[p] = row_sum(ratio, p, size, row_taps, -1)
        return 0

    lax.fori_loop(0, planes, sum_rows, 0, unroll=2)
    tail[...] = ratio[:, size : size + EDGE, :]
    for l in range(PLANE_HALF):
        low = unskewed(spread[l], PLANE_HALF + l)
        high = unskewed(spread[planes - PLANE_HALF + l], planes + l)
        pair[l] = jnp.where(odd, low, high)
        other[l] = jnp.where(odd, high, low)


def update_body(
    sends, begin, edges, place_of, taps, spread, left, right, high_w, low_w, est, turn, *refs
):
    refs = list(refs)
    before = [refs.pop(0) for _ in range(1 if begin else 0)]
    turned, outs = refs[0], refs[1:-3]
    sides, wide, back = refs[-3:]
    planes, rows, cols = turned.shape
    set_sides(sides, left, right, planes, (place_of[0] & 1) == 1)
    for l in range(planes):

        def tile(t, _, l=l):
            row = pl.multiple_of(t * 8, 8)
            wide[pl.ds(row, 8), :] = plane_sum(spread, row, sides, row, l, planes, taps, -1)
            return 0

        lax.fori_loop(0, rows // 8, tile, 0, unroll=True)
        back[l] = unskewed(wide[...], PLANE_HALF + l)
    x = back[...].reshape(planes * rows, cols)
    y = product(x, high_w[...], low_w[...], ((1,), (1,)))
    back[...] = y.reshape(planes, rows, cols)

    def rotate(t, _):
        row = pl.multiple_of(t * 8, 8)
        for c in range(0, cols, 2 * LANES):
            here = (pl.ds(row, 8), pl.ds(c, 2 * LANES))
            there = (pl.ds(begin + row, 8), pl.ds(c, 2 * LANES))
            field = [back[(p, *here)] * est[(p, *there)] for p in range(planes)]
            bits = jnp.broadcast_to(turn[:, c : c + 2 * LANES], (8, 2 * LANES))
            for bit in range((planes - 1).bit_length()):
                chosen = (bits >> bit & 1) == 1
                field = [
                    jnp.where(chosen, field[(q - (1 << bit)) % planes], field[q])
                    for q in range(planes)
                ]
            for q in range(planes):
                turned[(q, *here)] = field[q]
        return 0

    lax.fori_loop(0, rows // 8, rotate, 0, unroll=2)
    for (plan, ds, whole), out in zip(sends, outs):
        fields = fields_of(before + [turned] if whole else [turned], plan.part_rows)
        for i, (d, skip) in enumerate(ds):
            pack(plan, edges, d, skip, fields, out, i)


class Packing:
    def __init__(self, planes, cols, parts, part_rows, width):
        self.planes, self.cols, self.parts, self.width = planes, cols, parts, width
        self.part_rows = part_rows
        tiles = -(-parts * planes * width // LANES)
        self.shape = (tiles * part_rows, LANES)


def lane_of(shape):
    return lax.broadcasted_iota(jnp.int32, shape, 1)


def pack(plan, edges, d, skip, fields, out, slot):
    tall = range(0, plan.part_rows, 8)
    last = plan.cols // LANES - 1
    lane = lane_of((8, LANES))
    done = {}
    for k in range(plan.parts * plan.planes):
        h, q = divmod(k, plan.planes)
        field, base = fields[h]
        low = edges[d * plan.planes + q] + skip
        tile = low >> LANE_BITS
        one = pl.multiple_of(jnp.minimum(tile, last) << LANE_BITS, LANES)
        two = pl.multiple_of(jnp.minimum(tile + 1, last) << LANE_BITS, LANES)
        begin = k * plan.width
        target, offset = divmod(begin, LANES)
        turn = (offset - low) & (LANES - 1)
        split = lane >= (low & (LANES - 1))
        windows = []
        for t in tall:
            rows = pl.ds(base + t, 8)
            first, second = (field[q, rows, pl.ds(c, LANES)] for c in (one, two))
            windows.append(pltpu.roll(jnp.where(split, first, second), turn, 1))
        if offset == 0:
            done[target] = windows
        else:
            done[target] = [
                jnp.where(lane >= offset, x, y) for x, y in zip(windows, done[target])
            ]
        if offset + plan.width > LANES:
            done[target + 1] = windows
        end = k + 1 == plan.parts * plan.planes
        for full in [x for x in done if end or (x + 1) * LANES <= begin + plan.width]:
            for t, x in zip(tall, done.pop(full)):
                out[slot, pl.ds(full * plan.part_rows + t, 8), :] = x


def place(sources, edges, me, bases, out, first_round, begin):
    plan = sources[0][0]
    tall = range(0, plan.part_rows, 8)
    count = plan.cols // LANES
    lane = lane_of((8, LANES))
    spots = [(h, t) for h in range(len(bases)) for t in tall]
    for q in range(plan.planes):
        found = {}
        bound = edges[plan.planes + q]
        for c in range(count):
            keep = lane < bound - c * LANES
            for h, t in spots:
                base, row = bases[h]
                x = base[q, row + t : row + t + 8, c * LANES : (c + 1) * LANES]
                found[h, t, c] = jnp.where(keep, x, 0.0) if first_round else x
        for plan, message, slot, d, skip, first_part in sources:
            low = edges[d * plan.planes + q] + skip
            high = jnp.minimum(edges[(d + 1) * plan.planes + q], low + plan.width)
            high = jnp.where(me >= d, high, 0)
            inside = [(lane >= low - c * LANES) & (lane < high - c * LANES) for c in range(count)]
            for h in range(len(bases)):
                k = (first_part + h) * plan.planes + q
                target, offset = divmod(k * plan.width, LANES)
                turn = (low - offset) & (LANES - 1)
                for t in tall:
                    row = target * plan.part_rows + t
                    window = message[slot, pl.ds(row, 8), :]
                    if offset + plan.width > LANES:
                        after = message[slot, pl.ds(row + plan.part_rows, 8), :]
                        window = jnp.where(lane >= offset, window, after)
                    window = pltpu.roll(window, turn, 1)
                    for c in range(count):
                        found[h, t, c] = jnp.where(inside[c], window, found[h, t, c])
        for (h, t, c), x in found.items():
            row = begin + h * plan.part_rows + t
            out[q, row : row + 8, c * LANES : (c + 1) * LANES] = x


def fields_of(refs, part_rows):
    return [(ref, row) for ref in refs for row in range(0, ref.shape[1], part_rows)]


def settle_first(sends, edges, place_of, base, *refs):
    sources = [
        (plan, ref, i, d, skip, 0)
        for (plan, ds, _), ref in zip(sends, refs)
        for i, (d, skip) in enumerate(ds)
    ]
    fields = fields_of([base], sends[0][0].part_rows)
    place(sources, edges, place_of[0], fields, refs[-1], True, 0)


def settle_last(sends, edges, place_of, settled, base, *refs):
    out, begin = refs[-1], settled.shape[1]
    part_rows = sends[0][0].part_rows
    sources, late = [], []
    for (plan, ds, whole), ref in zip(sends, refs):
        for i, (d, skip) in enumerate(ds):
            if whole:
                late.append((plan, ref, i, d, skip, 0))
            sources.append((plan, ref, i, d, skip, begin // part_rows if whole else 0))
    me = place_of[0]
    place(late, edges, me, fields_of([settled], part_rows), out, False, 0)
    place(sources, edges, me, fields_of([base], part_rows), out, True, begin)


def round_pack_body(count, plan, rooms, edges, place_of, step, *refs):
    out, fields = refs[-1], fields_of(refs[:-1], plan.part_rows)
    for d in range(1, count):
        slot = lax.rem(place_of[0] + d, count)
        pack(plan, edges, d, rooms[d - 1] + step[0] * plan.width, fields, out, slot)


def round_place_body(count, plan, rooms, edges, place_of, step, base, message, out):
    me = place_of[0]
    sources = [
        (plan, message, lax.rem(me + count - d, count), d, rooms[d - 1] + step[0] * plan.width, 0)
        for d in range(1, count)
    ]
    place(sources, edges, me, fields_of([base], plan.part_rows), out, False, 0)


def swapped(x, axis, begin):
    ends = [(i, i + 1) for i in range(begin, lax.axis_size(axis) - 1, 2)]
    return lax.ppermute(x, axis, ends + [(j, i) for i, j in ends])


def like(*shape):
    return jax.ShapeDtypeStruct(shape, F32)


def on_device(observed, estimate, column_weights, plane_taps, row_taps, shear_planes):
    planes, rows, cols = estimate.shape
    count = lax.axis_size("scan")
    width = cols + LANES
    half = rows * 4 // 64 * 8
    chunks = [(0, half), (half, rows)]
    fresh = [(begin + EDGE if begin else 0, end + EDGE) for begin, end in chunks]
    reach = 2 * ROW_HALF

    strip = like(3 * ROW_HALF * planes, cols)
    me = jnp.stack([lax.axis_index("scan"), lax.axis_index("lat")]).astype(jnp.int32)
    pair, other = run(strip_body, (strip, strip), [SMEM, VMEM, VMEM], (me, estimate, observed))
    below = swapped(other, "lat", 1)
    above = swapped(pair, "lat", 0)
    levels = jnp.arange((count + 1) * planes, dtype=jnp.int32) - planes
    edges = jnp.sum(shear_planes[None, :] <= levels[:, None], axis=1, dtype=jnp.int32)
    turn = (shear_planes % planes)[None, :]

    weight = jax.ShapeDtypeStruct(column_weights.shape, BF16)
    mixed, high_w, low_w = run(
        own_body,
        (like(planes, rows, cols), weight, weight),
        [VMEM, VMEM],
        (estimate, column_weights),
    )
    tall, *rims = run(
        functools.partial(rim_body, fresh),
        (
            like(planes, rows + 2 * EDGE, cols),
            *(like(PLANE_HALF, e - b, cols) for b, e in fresh for _ in range(2)),
        ),
        [SMEM, VMEM, VMEM, VMEM, VMEM, VMEM, SMEM],
        (me, mixed, above, below, high_w, low_w, row_taps),
        [
            pltpu.VMEM((planes, 2 * EDGE, cols), F32),
            pltpu.VMEM((2, rows + EDGE, cols), F32),
        ],
    )
    framed = like(planes, rows + EDGE, width)
    blur, seen = run(
        frame_body,
        (framed, framed),
        [SMEM, VMEM, VMEM, VMEM, VMEM, SMEM],
        (me, tall, observed, above, below, row_taps),
        [pltpu.VMEM((rows + EDGE, cols), F32)],
    )

    def beside(pair, other):
        last = swapped(other, "scan", 1)
        return swapped(pair, "scan", 0), last

    def beside(pair, other):
        last = swapped(other, "scan", 1)
        return swapped(pair, "scan", 0), last

    def exchange(message):
        return lax.all_to_all(message, "scan", split_axis=0, concat_axis=0, tiled=True)

    share = max(cols // count, 8)
    part_rows = 16 if half % 16 == 0 and rows % 16 == 0 else 8

    def packing(height, columns):
        parts = height // part_rows
        return Packing(planes, cols, parts, part_rows, min(-(-columns // 8) * 8, LANES))

    near, far = packing(rows, share * 9 // 8), packing(rows, share * 3 // 2)
    later = packing(rows, share // 4)
    mids = []
    for begin, end in chunks:
        middle = packing(end - begin, share * 5 // 4)
        middle_first = sorted(range(2, count - 1), key=lambda d: abs(2 * d - count - 1))
        distances = middle_first if begin else range(2, count - 1)
        mids.append([(middle, [(d, 0)], False) for d in distances])
    wide = [
        (near, [(1, 0), (1, near.width)], True),
        (far, [(count - 1, 0)], True),
    ]
    rooms = [2 * near.width] + [middle.width] * (count - 3) + [far.width]

    tail = settled = None
    pieces = []
    left, right = beside(*rims[0:2])
    for i, (begin, end) in enumerate(chunks):
        size = end - begin
        last = i == len(chunks) - 1
        if pieces:
            left, right, pieces[-1] = lax.optimization_barrier((left, right, pieces[-1]))
        before = (tail,) if pieces else ()
        spread, low, high, tail = run(
            functools.partial(quotient_body, i == 0, begin, size),
            (
                like(planes, size, width),
                like(PLANE_HALF, size, cols),
                like(PLANE_HALF, size, cols),
                like(planes, EDGE, width),
            ),
            [SMEM, VMEM, VMEM, VMEM, VMEM, SMEM, SMEM] + [VMEM] * len(before),
            (me, blur, seen, left, right, plane_taps, row_taps, *before),
            [
                pltpu.VMEM((2 * PLANE_HALF, fresh[i][1] - fresh[i][0], width), F32),
                pltpu.VMEM((planes, size + EDGE, width), F32),
            ],
        )
        if last:
            heavy = [j for j, (_, ds, _) in enumerate(mids[0]) if abs(2 * ds[0][0] - count - 1) == 1]
            rest = [j for j in range(len(mids[0])) if j not in heavy]
            low, high, early = lax.optimization_barrier((low, high, [moved[j] for j in heavy]))
            sides = beside(low, high)
            sides, late = lax.optimization_barrier((sides, [moved[j] for j in rest]))
            moved = [None] * len(mids[0])
            for j, x in zip(heavy + rest, early + late):
                moved[j] = x
            settled = run(
                functools.partial(settle_first, mids[0]),
                like(planes, begin, cols),
                [SMEM, SMEM] + [VMEM] * (1 + len(moved)),
                (edges, me, pieces[0], *moved),
            )
        else:
            ahead = lax.optimization_barrier((low, high, *rims[2 * i + 2 : 2 * i + 4]))
            sides = beside(*ahead[:2])
            left, right = beside(*ahead[2:])
        sends = mids[i] + wide if last else mids[i]
        turned, *packed = run(
            functools.partial(update_body, sends, begin),
            (
                like(planes, size, cols),
                *(like(len(ds), *plan.shape) for plan, ds, _ in sends),
            ),
            [SMEM, SMEM, SMEM] + [VMEM] * (7 + len(pieces)),
            (edges, me, plane_taps, spread, *sides, high_w, low_w, estimate, turn, *pieces),
            [
                pltpu.VMEM((2 * PLANE_HALF, size, width), F32),
                pltpu.VMEM((size, width), F32),
                pltpu.VMEM((planes, size, cols), F32),
            ],
        )
        pieces.append(turned)
        moved = [
            lax.ppermute(x, "scan", [(j, j + ds[0][0]) for j in range(count - ds[0][0])])
            for (_, ds, _), x in zip(sends, packed)
        ]
    settled = run(
        functools.partial(settle_last, sends),
        like(planes, rows, cols),
        [SMEM, SMEM] + [VMEM] * (2 + len(moved)),
        (edges, me, settled, turned, *moved),
    )

    table = edges.reshape(count + 1, planes)
    row = lax.broadcasted_iota(jnp.int32, (count - 1, planes), 0)
    room = jnp.where(row == 0, rooms[0], jnp.where(row == count - 2, rooms[-1], middle.width))
    rest = table[2:] - table[1:-1] - room
    rounds = jnp.max((rest + later.width - 1) // later.width)

    def again(state):
        step = state[0][None]
        message = run(
            functools.partial(round_pack_body, count, later, rooms),
            like(count, *later.shape),
            [SMEM, SMEM, SMEM] + [VMEM] * len(pieces),
            (edges, me, step, *pieces),
        )
        base = run(
            functools.partial(round_place_body, count, later, rooms),
            like(planes, rows, cols),
            [SMEM, SMEM, SMEM, VMEM, VMEM],
            (edges, me, step, state[1], exchange(message)),
        )
        return state[0] + 1, base

    return lax.while_loop(lambda state: state[0] < rounds, again, (jnp.int32(0), settled))[1]


def solution(mesh):
    placed = (P("scan", "lat", None), P("scan", "lat", None), P(), P(), P(), P())
    return jax.shard_map(
        on_device, mesh=mesh, in_specs=placed, out_specs=P("scan", "lat", None), check_vma=False
    )
```

```python
import functools

import jax
import jax.numpy as jnp
from jax import lax
from jax.experimental import pallas as pl
from jax.experimental.pallas import tpu as pltpu
from jax.sharding import PartitionSpec as P

PLANE_HALF = 3
ROW_HALF = 3
SKEW = 2
LANES = 128
LANE_BITS = 7
EDGE = 8
F32 = jnp.float32
BF16 = jnp.bfloat16
VMEM = pl.BlockSpec(memory_space=pltpu.VMEM)
SMEM = pl.BlockSpec(memory_space=pltpu.SMEM)
LIMIT = 20 * 1024 * 1024


def run(body, outs, ins, operands, scratch=(), aliases=None, cost=None):
    return pl.pallas_call(
        body,
        out_shape=outs,
        in_specs=ins,
        out_specs=jax.tree.map(lambda _: VMEM, outs),
        scratch_shapes=list(scratch),
        input_output_aliases=aliases or {},
        compiler_params=pltpu.CompilerParams(vmem_limit_bytes=LIMIT),
        cost_estimate=cost,
    )(*operands)


def halves(x):
    high = x.astype(BF16)
    return high, (x - high.astype(F32)).astype(BF16)


def product(x, high_w, low_w, dims):
    high, low = halves(x)
    dot = functools.partial(
        lax.dot_general, dimension_numbers=(dims, ((), ())), preferred_element_type=F32
    )
    return dot(high, high_w) + (dot(high, low_w) + dot(low, high_w))


def row_sum(field, plane, rows, taps, direction):
    total = None
    for k in range(2 * ROW_HALF + 1):
        tap = taps[k] if direction > 0 else taps[2 * ROW_HALF - k]
        term = tap * field[plane, pl.ds(k, rows), :]
        total = term if total is None else total + term
    return total


def strip_body(place_of, est, observed, pair, other):
    planes, rows, cols = est.shape
    reach = 2 * ROW_HALF
    odd = (place_of[1] & 1) == 1

    def put(begin, size, upper, lower):
        pair[begin : begin + size, :] = jnp.where(odd, upper, lower)
        other[begin : begin + size, :] = jnp.where(odd, lower, upper)

    for l in range(planes):
        put(l * reach, reach, est[l, 0:reach, :], est[l, rows - reach : rows, :])
        seen = observed[l].astype(F32)
        seek = (2 * planes + l) * ROW_HALF
        put(seek, ROW_HALF, seen[0:ROW_HALF], seen[rows - ROW_HALF : rows])


def own_body(est, weights, mixed, high_w, low_w):
    planes, rows, cols = est.shape
    high, low = halves(weights[...])
    high_w[...] = high
    low_w[...] = low
    x = est[...].reshape(planes * rows, cols)
    mixed[...] = product(x, high, low, ((1,), (0,))).reshape(planes, rows, cols)


def rim_body(chunks, place_of, mixed, pair, other, high_w, low_w, taps, tall, *refs):
    rims, ends, edge = refs[:-2], refs[-2], refs[-1]
    odd = (place_of[0] & 1) == 1
    planes, rows, cols = mixed.shape
    reach = 2 * ROW_HALF
    ends[...] = jnp.zeros(ends.shape, F32)
    odd_row = (place_of[1] & 1) == 1
    for l in range(planes):
        x, y = pair[l * reach : (l + 1) * reach, :], other[l * reach : (l + 1) * reach, :]
        ends[l, 0:reach, :] = jnp.where(odd_row, x, y)
        ends[l, EDGE : EDGE + reach, :] = jnp.where(odd_row, y, x)
    x = ends[...].reshape(planes * 2 * EDGE, cols)
    ends[...] = product(x, high_w[...], low_w[...], ((1,), (0,))).reshape(ends.shape)
    tall[:, 0:reach, :] = ends[:, 0:reach, :]
    tall[:, reach : reach + rows, :] = mixed[...]
    tall[:, reach + rows : reach + rows + EDGE, :] = ends[:, EDGE:, :]
    tall[:, reach + rows + EDGE :, :] = jnp.zeros((planes, EDGE - reach, cols), F32)
    for l in range(PLANE_HALF):
        for side, base in enumerate((0, planes - PLANE_HALF)):
            edge[side] = row_sum(tall, base + l, rows + EDGE, taps, 1)
        for i, (begin, end) in enumerate(chunks):
            low, high = edge[0, begin:end, :], edge[1, begin:end, :]
            rims[2 * i][l] = jnp.where(odd, low, high)
            rims[2 * i + 1][l] = jnp.where(odd, high, low)


def frame_body(place_of, tall, observed, pair, other, taps, blur, seen, frame):
    planes, rows, cols = observed.shape
    for l in range(planes):
        blur[l] = skewed(row_sum(tall, l, rows + EDGE, taps, 1), PLANE_HALF + l)
    frame[...] = jnp.zeros(frame.shape, F32)
    odd = (place_of[1] & 1) == 1
    for l in range(planes):
        seek = (2 * planes + l) * ROW_HALF
        x, y = pair[seek : seek + ROW_HALF, :], other[seek : seek + ROW_HALF, :]
        frame[0:ROW_HALF, :] = jnp.where(odd, x, y)
        frame[ROW_HALF : ROW_HALF + rows, :] = observed[l].astype(F32)
        frame[ROW_HALF + rows : 2 * ROW_HALF + rows, :] = jnp.where(odd, y, x)
        seen[l] = skewed(frame[...], PLANE_HALF + l)


def skewed(x, place):
    rows, cols = x.shape
    wide = jnp.concatenate([x, jnp.zeros((rows, LANES), F32)], axis=1)
    return pltpu.roll(wide, SKEW * place, 1) if place else wide


def unskewed(x, place):
    width = x.shape[1]
    moved = pltpu.roll(x, (width - SKEW * place) % width, 1) if place else x
    return moved[:, : width - LANES]


def set_sides(sides, pair, other, planes, odd):
    for l in range(PLANE_HALF):
        x, y = pair[l], other[l]
        sides[l] = skewed(jnp.where(odd, x, y), l)
        sides[PLANE_HALF + l] = skewed(jnp.where(odd, y, x), planes + PLANE_HALF + l)


def plane_sum(own, own_row, sides, row, plane, planes, taps, direction):
    total = None
    for k in range(2 * PLANE_HALF + 1):
        source = plane + k - PLANE_HALF
        if source < 0:
            x = sides[source + PLANE_HALF, pl.ds(row, 8), :]
        elif source >= planes:
            x = sides[source - planes + PLANE_HALF, pl.ds(row, 8), :]
        else:
            x = own[source, pl.ds(own_row, 8), :]
        term = (taps[k] if direction > 0 else taps[2 * PLANE_HALF - k]) * x
        total = term if total is None else total + term
    return total


def quotient_body(first, begin, size, place_of, blur, seen, left, right, plane_taps, row_taps, *refs):
    odd = (place_of[0] & 1) == 1
    refs = list(refs)
    before = None if first else refs.pop(0)
    spread, pair, other, tail, sides, ratio = refs
    planes = blur.shape[0]
    fresh = 0 if first else EDGE
    if not first:
        ratio[:, 0:EDGE, :] = before[...]
    set_sides(sides, left, right, planes, odd)
    for l in range(planes):

        def tile(t, _, l=l):
            row = pl.multiple_of(t * 8, 8)
            there = pl.multiple_of(row + begin + fresh, 8)
            blurred = plane_sum(blur, there, sides, row, l, planes, plane_taps, 1)
            ratio[l, pl.ds(pl.multiple_of(row + fresh, 8), 8), :] = seen[
                l, pl.ds(there, 8), :
            ] / jnp.where(blurred > 0, blurred, 1.0)
            return 0

        lax.fori_loop(0, (size + EDGE - fresh) // 8, tile, 0, unroll=True)

    def sum_rows(p, _):
        spread[p] = row_sum(ratio, p, size, row_taps, -1)
        return 0

    lax.fori_loop(0, planes, sum_rows, 0, unroll=2)
    tail[...] = ratio[:, size : size + EDGE, :]
    for l in range(PLANE_HALF):
        low = unskewed(spread[l], PLANE_HALF + l)
        high = unskewed(spread[planes - PLANE_HALF + l], planes + l)
        pair[l] = jnp.where(odd, low, high)
        other[l] = jnp.where(odd, high, low)


def update_body(
    sends, begin, edges, place_of, taps, spread, left, right, high_w, low_w, est, turn, *refs
):
    refs = list(refs)
    before = [refs.pop(0) for _ in range(1 if begin else 0)]
    turned, outs = refs[0], refs[1:-3]
    sides, wide, back = refs[-3:]
    planes, rows, cols = turned.shape
    set_sides(sides, left, right, planes, (place_of[0] & 1) == 1)
    for l in range(planes):

        def tile(t, _, l=l):
            row = pl.multiple_of(t * 8, 8)
            wide[pl.ds(row, 8), :] = plane_sum(spread, row, sides, row, l, planes, taps, -1)
            return 0

        lax.fori_loop(0, rows // 8, tile, 0, unroll=True)
        back[l] = unskewed(wide[...], PLANE_HALF + l)
    x = back[...].reshape(planes * rows, cols)
    y = product(x, high_w[...], low_w[...], ((1,), (1,)))
    back[...] = y.reshape(planes, rows, cols)

    def rotate(t, _):
        row = pl.multiple_of(t * 8, 8)
        for c in range(0, cols, 2 * LANES):
            here = (pl.ds(row, 8), pl.ds(c, 2 * LANES))
            there = (pl.ds(begin + row, 8), pl.ds(c, 2 * LANES))
            field = [back[(p, *here)] * est[(p, *there)] for p in range(planes)]
            bits = jnp.broadcast_to(turn[:, c : c + 2 * LANES], (8, 2 * LANES))
            for bit in range((planes - 1).bit_length()):
                chosen = (bits >> bit & 1) == 1
                field = [
                    jnp.where(chosen, field[(q - (1 << bit)) % planes], field[q])
                    for q in range(planes)
                ]
            for q in range(planes):
                turned[(q, *here)] = field[q]
        return 0

    lax.fori_loop(0, rows // 8, rotate, 0, unroll=2)
    for (plan, ds, whole), out in zip(sends, outs):
        fields = fields_of(before + [turned] if whole else [turned], plan.part_rows)
        for i, (d, skip) in enumerate(ds):
            pack(plan, edges, d, skip, fields, out, i)


class Packing:
    def __init__(self, planes, cols, parts, part_rows, width):
        self.planes, self.cols, self.parts, self.width = planes, cols, parts, width
        self.part_rows = part_rows
        tiles = -(-parts * planes * width // LANES)
        self.shape = (tiles * part_rows, LANES)


def lane_of(shape):
    return lax.broadcasted_iota(jnp.int32, shape, 1)


def pack(plan, edges, d, skip, fields, out, slot):
    tall = range(0, plan.part_rows, 8)
    last = plan.cols // LANES - 1
    lane = lane_of((8, LANES))
    done = {}
    for k in range(plan.parts * plan.planes):
        h, q = divmod(k, plan.planes)
        field, base = fields[h]
        low = edges[d * plan.planes + q] + skip
        tile = low >> LANE_BITS
        one = pl.multiple_of(jnp.minimum(tile, last) << LANE_BITS, LANES)
        two = pl.multiple_of(jnp.minimum(tile + 1, last) << LANE_BITS, LANES)
        begin = k * plan.width
        target, offset = divmod(begin, LANES)
        turn = (offset - low) & (LANES - 1)
        split = lane >= (low & (LANES - 1))
        windows = []
        for t in tall:
            rows = pl.ds(base + t, 8)
            first, second = (field[q, rows, pl.ds(c, LANES)] for c in (one, two))
            windows.append(pltpu.roll(jnp.where(split, first, second), turn, 1))
        if offset == 0:
            done[target] = windows
        else:
            done[target] = [
                jnp.where(lane >= offset, x, y) for x, y in zip(windows, done[target])
            ]
        if offset + plan.width > LANES:
            done[target + 1] = windows
        end = k + 1 == plan.parts * plan.planes
        for full in [x for x in done if end or (x + 1) * LANES <= begin + plan.width]:
            for t, x in zip(tall, done.pop(full)):
                out[slot, pl.ds(full * plan.part_rows + t, 8), :] = x


def place(sources, edges, me, bases, out, first_round, begin):
    plan = sources[0][0]
    tall = range(0, plan.part_rows, 8)
    count = plan.cols // LANES
    lane = lane_of((8, LANES))
    spots = [(h, t) for h in range(len(bases)) for t in tall]
    for q in range(plan.planes):
        found = {}
        bound = edges[plan.planes + q]
        for c in range(count):
            keep = lane < bound - c * LANES
            for h, t in spots:
                base, row = bases[h]
                x = base[q, row + t : row + t + 8, c * LANES : (c + 1) * LANES]
                found[h, t, c] = jnp.where(keep, x, 0.0) if first_round else x
        for plan, message, slot, d, skip, first_part in sources:
            low = edges[d * plan.planes + q] + skip
            high = jnp.minimum(edges[(d + 1) * plan.planes + q], low + plan.width)
            high = jnp.where(me >= d, high, 0)
            inside = [(lane >= low - c * LANES) & (lane < high - c * LANES) for c in range(count)]
            for h in range(len(bases)):
                k = (first_part + h) * plan.planes + q
                target, offset = divmod(k * plan.width, LANES)
                turn = (low - offset) & (LANES - 1)
                for t in tall:
                    row = target * plan.part_rows + t
                    window = message[slot, pl.ds(row, 8), :]
                    if offset + plan.width > LANES:
                        after = message[slot, pl.ds(row + plan.part_rows, 8), :]
                        window = jnp.where(lane >= offset, window, after)
                    window = pltpu.roll(window, turn, 1)
                    for c in range(count):
                        found[h, t, c] = jnp.where(inside[c], window, found[h, t, c])
        for (h, t, c), x in found.items():
            row = begin + h * plan.part_rows + t
            out[q, row : row + 8, c * LANES : (c + 1) * LANES] = x


def fields_of(refs, part_rows):
    return [(ref, row) for ref in refs for row in range(0, ref.shape[1], part_rows)]


def settle_first(sends, edges, place_of, base, *refs):
    sources = [
        (plan, ref, i, d, skip, 0)
        for (plan, ds, _), ref in zip(sends, refs)
        for i, (d, skip) in enumerate(ds)
    ]
    fields = fields_of([base], sends[0][0].part_rows)
    place(sources, edges, place_of[0], fields, refs[-1], True, 0)


def settle_last(sends, edges, place_of, settled, base, *refs):
    out, begin = refs[-1], settled.shape[1]
    part_rows = sends[0][0].part_rows
    sources, late = [], []
    for (plan, ds, whole), ref in zip(sends, refs):
        for i, (d, skip) in enumerate(ds):
            if whole:
                late.append((plan, ref, i, d, skip, 0))
            sources.append((plan, ref, i, d, skip, begin // part_rows if whole else 0))
    me = place_of[0]
    place(late, edges, me, fields_of([settled], part_rows), out, False, 0)
    place(sources, edges, me, fields_of([base], part_rows), out, True, begin)


def round_pack_body(count, plan, rooms, edges, place_of, step, *refs):
    out, fields = refs[-1], fields_of(refs[:-1], plan.part_rows)
    for d in range(1, count):
        slot = lax.rem(place_of[0] + d, count)
        pack(plan, edges, d, rooms[d - 1] + step[0] * plan.width, fields, out, slot)


def round_place_body(count, plan, rooms, edges, place_of, step, base, message, out):
    me = place_of[0]
    sources = [
        (plan, message, lax.rem(me + count - d, count), d, rooms[d - 1] + step[0] * plan.width, 0)
        for d in range(1, count)
    ]
    place(sources, edges, me, fields_of([base], plan.part_rows), out, False, 0)


def swapped(x, axis, begin):
    ends = [(i, i + 1) for i in range(begin, lax.axis_size(axis) - 1, 2)]
    return lax.ppermute(x, axis, ends + [(j, i) for i, j in ends])


def like(*shape):
    return jax.ShapeDtypeStruct(shape, F32)


def on_device(observed, estimate, column_weights, plane_taps, row_taps, shear_planes):
    planes, rows, cols = estimate.shape
    count = lax.axis_size("scan")
    width = cols + LANES
    half = rows * 4 // 64 * 8
    chunks = [(0, half), (half, rows)]
    fresh = [(begin + EDGE if begin else 0, end + EDGE) for begin, end in chunks]
    reach = 2 * ROW_HALF

    strip = like(3 * ROW_HALF * planes, cols)
    me = jnp.stack([lax.axis_index("scan"), lax.axis_index("lat")]).astype(jnp.int32)
    pair, other = run(strip_body, (strip, strip), [SMEM, VMEM, VMEM], (me, estimate, observed))
    above = swapped(pair, "lat", 0)
    below = swapped(other, "lat", 1)
    levels = jnp.arange((count + 1) * planes, dtype=jnp.int32) - planes
    edges = jnp.sum(shear_planes[None, :] <= levels[:, None], axis=1, dtype=jnp.int32)
    turn = (shear_planes % planes)[None, :]

    weight = jax.ShapeDtypeStruct(column_weights.shape, BF16)
    mixed, high_w, low_w = run(
        own_body,
        (like(planes, rows, cols), weight, weight),
        [VMEM, VMEM],
        (estimate, column_weights),
    )
    tall, *rims = run(
        functools.partial(rim_body, fresh),
        (
            like(planes, rows + 2 * EDGE, cols),
            *(like(PLANE_HALF, e - b, cols) for b, e in fresh for _ in range(2)),
        ),
        [SMEM, VMEM, VMEM, VMEM, VMEM, VMEM, SMEM],
        (me, mixed, above, below, high_w, low_w, row_taps),
        [
            pltpu.VMEM((planes, 2 * EDGE, cols), F32),
            pltpu.VMEM((2, rows + EDGE, cols), F32),
        ],
    )
    framed = like(planes, rows + EDGE, width)
    blur, seen = run(
        frame_body,
        (framed, framed),
        [SMEM, VMEM, VMEM, VMEM, VMEM, SMEM],
        (me, tall, observed, above, below, row_taps),
        [pltpu.VMEM((rows + EDGE, cols), F32)],
    )

    def beside(pair, other):
        last = swapped(other, "scan", 1)
        return swapped(pair, "scan", 0), last

    def beside(pair, other):
        last = swapped(other, "scan", 1)
        return swapped(pair, "scan", 0), last

    def exchange(message):
        return lax.all_to_all(message, "scan", split_axis=0, concat_axis=0, tiled=True)

    share = max(cols // count, 8)
    part_rows = 16 if half % 16 == 0 and rows % 16 == 0 else 8

    def packing(height, columns):
        parts = height // part_rows
        return Packing(planes, cols, parts, part_rows, min(-(-columns // 8) * 8, LANES))

    near, far = packing(rows, share), packing(rows, share * 3 // 2)
    later = packing(rows, share // 4)
    mids = []
    for begin, end in chunks:
        middle = packing(end - begin, share * 5 // 4)
        middle_first = sorted(range(2, count - 1), key=lambda d: abs(2 * d - count - 1))
        distances = middle_first if begin else range(2, count - 1)
        mids.append([(middle, [(d, 0)], False) for d in distances])
    wide = [
        (near, [(1, 0), (1, near.width)], True),
        (far, [(count - 1, 0)], True),
    ]
    rooms = [2 * near.width] + [middle.width] * (count - 3) + [far.width]

    tail = settled = None
    pieces = []
    left, right = beside(*rims[0:2])
    for i, (begin, end) in enumerate(chunks):
        size = end - begin
        last = i == len(chunks) - 1
        if pieces:
            left, right, pieces[-1] = lax.optimization_barrier((left, right, pieces[-1]))
        before = (tail,) if pieces else ()
        spread, low, high, tail = run(
            functools.partial(quotient_body, i == 0, begin, size),
            (
                like(planes, size, width),
                like(PLANE_HALF, size, cols),
                like(PLANE_HALF, size, cols),
                like(planes, EDGE, width),
            ),
            [SMEM, VMEM, VMEM, VMEM, VMEM, SMEM, SMEM] + [VMEM] * len(before),
            (me, blur, seen, left, right, plane_taps, row_taps, *before),
            [
                pltpu.VMEM((2 * PLANE_HALF, fresh[i][1] - fresh[i][0], width), F32),
                pltpu.VMEM((planes, size + EDGE, width), F32),
            ],
        )
        if last:
            heavy = [j for j, (_, ds, _) in enumerate(mids[0]) if abs(2 * ds[0][0] - count - 1) == 1]
            rest = [j for j in range(len(mids[0])) if j not in heavy]
            low, high, early = lax.optimization_barrier((low, high, [moved[j] for j in heavy]))
            sides = beside(low, high)
            sides, late = lax.optimization_barrier((sides, [moved[j] for j in rest]))
            moved = [None] * len(mids[0])
            for j, x in zip(heavy + rest, early + late):
                moved[j] = x
            settled = run(
                functools.partial(settle_first, mids[0]),
                like(planes, begin, cols),
                [SMEM, SMEM] + [VMEM] * (1 + len(moved)),
                (edges, me, pieces[0], *moved),
            )
        else:
            ahead = lax.optimization_barrier((low, high, *rims[2 * i + 2 : 2 * i + 4]))
            sides = beside(*ahead[:2])
            left, right = beside(*ahead[2:])
        sends = mids[i] + wide if last else mids[i]
        turned, *packed = run(
            functools.partial(update_body, sends, begin),
            (
                like(planes, size, cols),
                *(like(len(ds), *plan.shape) for plan, ds, _ in sends),
            ),
            [SMEM, SMEM, SMEM] + [VMEM] * (7 + len(pieces)),
            (edges, me, plane_taps, spread, *sides, high_w, low_w, estimate, turn, *pieces),
            [
                pltpu.VMEM((2 * PLANE_HALF, size, width), F32),
                pltpu.VMEM((size, width), F32),
                pltpu.VMEM((planes, size, cols), F32),
            ],
        )
        pieces.append(turned)
        moved = [
            lax.ppermute(x, "scan", [(j, j + ds[0][0]) for j in range(count - ds[0][0])])
            for (_, ds, _), x in zip(sends, packed)
        ]
    settled = run(
        functools.partial(settle_last, sends),
        like(planes, rows, cols),
        [SMEM, SMEM] + [VMEM] * (2 + len(moved)),
        (edges, me, settled, turned, *moved),
    )

    table = edges.reshape(count + 1, planes)
    row = lax.broadcasted_iota(jnp.int32, (count - 1, planes), 0)
    room = jnp.where(row == 0, rooms[0], jnp.where(row == count - 2, rooms[-1], middle.width))
    rest = table[2:] - table[1:-1] - room
    rounds = jnp.max((rest + later.width - 1) // later.width)

    def again(state):
        step = state[0][None]
        message = run(
            functools.partial(round_pack_body, count, later, rooms),
            like(count, *later.shape),
            [SMEM, SMEM, SMEM] + [VMEM] * len(pieces),
            (edges, me, step, *pieces),
        )
        base = run(
            functools.partial(round_place_body, count, later, rooms),
            like(planes, rows, cols),
            [SMEM, SMEM, SMEM, VMEM, VMEM],
            (edges, me, step, state[1], exchange(message)),
        )
        return state[0] + 1, base

    return lax.while_loop(lambda state: state[0] < rounds, again, (jnp.int32(0), settled))[1]


def solution(mesh):
    placed = (P("scan", "lat", None), P("scan", "lat", None), P(), P(), P(), P())
    return jax.shard_map(
        on_device, mesh=mesh, in_specs=placed, out_specs=P("scan", "lat", None), check_vma=False
    )
```
